256 devices in a mesh: dp: 4 (over z_hi), mx: 16 (over z_lo, y, core), my: 4 (over x).
Axes of the slice: x: 4, y: 4, z: 8 (z_hi: 4, z_lo: 2; z = z_hi * 2 + z_lo), core: 2. Of those that a mesh axis runs over, the one named last changes fastest.
Arguments:
- inputs: bfloat16 [1024, 6144], P(('dp', 'my'), 'mx'), may hold values from -18 to 18
- triple_weight: bfloat16 [6144, 3, 6144], P('mx', None, 'my'), may hold values from -0.078125 to 0.078125
- expand_weight: bfloat16 [6144, 12288], P('mx', 'my'), may hold values from -0.078125 to 0.078125
- merge_weight: bfloat16 [6144, 6144], P('mx', 'my'), may hold values from -0.078125 to 0.078125
- shrink_weight: bfloat16 [6144, 12288], P('mx', 'my'), may hold values from -0.0546875 to 0.0546875
- cotangent: bfloat16 [1024, 6144], P(('dp', 'my'), 'mx'), may hold values from -4 to 4
Outputs:
- outputs: bfloat16 [1024, 6144], P(('dp', 'my'), 'mx')
- block_input_gradient: bfloat16 [1024, 6144], P(('dp', 'my'), 'mx')
- triple_grad: bfloat16 [6144, 3, 6144], P(('mx', 'dp'), None, 'my')
- expand_grad: bfloat16 [6144, 12288], P(('mx', 'dp'), 'my')
- merge_grad: bfloat16 [6144, 6144], P(('mx', 'dp'), 'my')
- shrink_grad: bfloat16 [6144, 12288], P(('mx', 'dp'), 'my')
The draws below stay inside these ranges and needn't reach their ends.
All inputs are finite; a program needn't handle non-finite values.
Results may differ from the reference program's by a relative error of at most 0.04.
Values may be sent and summed in bfloat16 or wider, within the bound.
A program may use at most 128 MiB of HBM per device.

```python
import math
import jax
import jax.numpy as jnp
from jax import lax

MODEL_WIDTH = 6144
HEADS = 48
HEAD_DIM = 128
FF = 12288
PATCHES = 256
HID = 6144
GROUP = 256
REPLICAS = 4
ROWS = 1024
BLOCKS = 16
BLOCK_FEAT = 384


def draw_inputs(key, part):
    key = jax.random.fold_in(key, 11)
    keys = jax.random.split(key, 3)
    columns = jnp.arange(MODEL_WIDTH, dtype=jnp.float32) / MODEL_WIDTH
    column_scale = 3.0 ** columns * jax.random.uniform(keys[1], (MODEL_WIDTH,), jnp.float32, 0.6, 1.4)
    base = jnp.clip(jax.random.normal(keys[0], (ROWS, MODEL_WIDTH), jnp.float32), -4.0, 4.0)
    row_scale = 2.0 ** jax.random.uniform(keys[2], (ROWS, 1), jnp.float32)
    drawn = base * column_scale[None, :] * row_scale * 0.5
    return drawn.astype(jnp.bfloat16)


def block_levels(own_key, extent, cuts, low, high):
    gain = 1.0
    for axis_at, blocks in cuts:
        heights = jax.random.uniform(jax.random.fold_in(jax.random.fold_in(own_key, 6), axis_at), (blocks,), jnp.float32, low / len(cuts), high / len(cuts))
        gain = gain * jnp.repeat(jnp.exp(heights), extent[axis_at] // blocks).reshape((-1,) + (1,) * (len(extent) - 1 - axis_at))
    return gain


def bell_draw(rng, dims, scale, limit, shards=(), held_as=jnp.bfloat16):
    values = jax.random.normal(rng, dims, jnp.float32) * scale
    if len(shards) > 0:
        values = block_levels(rng, dims, shards, -0.22, 0.18) * values
    return jnp.clip(values, min=-limit, max=limit).astype(held_as)


def setup_inputs(seed: int = 0) -> dict:
    arg_keys = jax.random.split(jax.random.key(seed), 7)
    return {
        "inputs": draw_inputs(jax.random.fold_in(arg_keys[6], 71), 0),
        "triple_weight": bell_draw(arg_keys[1], (MODEL_WIDTH, 3, HID), MODEL_WIDTH ** -0.5, 0.078125, ((0, 16), (2, 4))),
        "expand_weight": bell_draw(arg_keys[2], (MODEL_WIDTH, FF), MODEL_WIDTH ** -0.5, 0.078125, ((0, 16), (1, 4))),
        "merge_weight": bell_draw(arg_keys[3], (MODEL_WIDTH, HID), HID ** -0.5, 0.078125, ((0, 16), (1, 4))),
        "shrink_weight": bell_draw(arg_keys[4], (MODEL_WIDTH, FF), FF ** -0.5, 0.0546875, ((0, 16), (1, 4))),
        "cotangent": bell_draw(arg_keys[5], (ROWS, MODEL_WIDTH), 0.25, 4.0, ((0, 16), (1, 16))),
    }


EPS = 1e-06
ROOT_HALF = 0.7071067811865476
INV_ROOT_TAU = 0.3989422804014327

def rounded(block):
    return lax.optimization_barrier(block.astype(jnp.bfloat16)).astype(jnp.float32)

def apply_layer_norm(block):
    centre = block - lax.optimization_barrier(jnp.mean(block, axis=-1, keepdims=True))
    inverse = lax.rsqrt(lax.optimization_barrier(jnp.mean(centre * centre, axis=-1, keepdims=True)) + EPS)
    return (centre * inverse, inverse)

def layer_norm_backward(grad_in, unit, inverse):
    first_mean = lax.optimization_barrier(jnp.mean(grad_in, axis=-1, keepdims=True))
    second_mean = lax.optimization_barrier(jnp.mean(grad_in * unit, axis=-1, keepdims=True))
    return (grad_in - first_mean - unit * second_mean) * inverse

def gelu_slope(pre_act):
    return 0.5 * (1.0 + lax.erf(pre_act * ROOT_HALF)) + pre_act * jnp.exp(-0.5 * pre_act * pre_act) * INV_ROOT_TAU

def blocked(left, right):
    width = right.shape[1]
    left_blocks = left.reshape(ROWS, BLOCKS, BLOCK_FEAT).transpose(1, 0, 2)
    right_blocks = right.reshape(BLOCKS, BLOCK_FEAT, width)

    def step(carry, pair):
        part = jnp.dot(pair[0], pair[1], preferred_element_type=jnp.float32)
        return (carry + rounded(part), None)
    start_acc = jnp.zeros((ROWS, width), jnp.float32)
    result, unused = lax.scan(step, start_acc, (left_blocks, right_blocks))
    return result

def replica_sum(left, right):
    left_parts = left.reshape(REPLICAS, GROUP, left.shape[1])
    right_parts = right.reshape(REPLICAS, GROUP, right.shape[1])

    def step(carry, pair):
        part = lax.dot_general(pair[0], pair[1], (((0,), (0,)), ((), ())), preferred_element_type=jnp.float32)
        return (carry + rounded(part), None)
    start_acc = jnp.zeros((left.shape[1], right.shape[1]), jnp.float32)
    result, unused = lax.scan(step, start_acc, (left_parts, right_parts))
    return result.astype(jnp.bfloat16)

def reference(inputs, triple_weight, expand_weight, merge_weight, shrink_weight, cotangent):
    input_float_rows = inputs.astype(jnp.float32)
    centered_scaled_input, inverse_row_deviation = apply_layer_norm(input_float_rows)
    normed_rows = centered_scaled_input.astype(jnp.bfloat16)
    joined = triple_weight.reshape(MODEL_WIDTH, 3 * HID)
    projected = blocked(normed_rows, joined)
    pre_act = blocked(normed_rows, expand_weight)
    images = ROWS // PATCHES
    shape_four = (images, PATCHES, HEADS, HEAD_DIM)
    qhat, q_inverse = apply_layer_norm(projected[:, :HID].reshape(shape_four))
    khat, k_inverse = apply_layer_norm(projected[:, HID:2 * HID].reshape(shape_four))
    q_norm = rounded(qhat)
    k_norm = rounded(khat)
    values = rounded(projected[:, 2 * HID:].reshape(shape_four))
    scale_factor = 1.0 / math.sqrt(HEAD_DIM)
    scores = jnp.einsum('iqhd,ikhd->ihqk', q_norm, k_norm) * scale_factor
    expo = jnp.exp(scores)
    probs = expo / lax.optimization_barrier(jnp.sum(expo, axis=-1, keepdims=True))
    probs_half = rounded(probs)
    attended = jnp.einsum('ihqk,ikhd->iqhd', probs_half, values).reshape(ROWS, HID).astype(jnp.bfloat16)
    hidden = jax.nn.gelu(pre_act, approximate=False).astype(jnp.bfloat16)
    branch = jnp.dot(attended, merge_weight.T, preferred_element_type=jnp.float32)
    branch = branch + jnp.dot(hidden, shrink_weight.T, preferred_element_type=jnp.float32)
    outputs = (input_float_rows + branch).astype(jnp.bfloat16)
    d_attended = rounded(blocked(cotangent, merge_weight)).reshape(shape_four)
    d_hidden = blocked(cotangent, shrink_weight)
    d_probs = jnp.einsum('iqhd,ikhd->ihqk', d_attended, values)
    d_scores = probs * (d_probs - lax.optimization_barrier(jnp.sum(probs * d_probs, axis=-1, keepdims=True)))
    d_scores_half = rounded(d_scores)
    d_qn = jnp.einsum('ihqk,ikhd->iqhd', d_scores_half, k_norm) * scale_factor
    d_kn = jnp.einsum('ihqk,iqhd->ikhd', d_scores_half, q_norm) * scale_factor
    d_values = jnp.einsum('ihqk,iqhd->ikhd', probs_half, d_attended)
    d_query = layer_norm_backward(d_qn, qhat, q_inverse).reshape(ROWS, HID)
    d_key = layer_norm_backward(d_kn, khat, k_inverse).reshape(ROWS, HID)
    d_joined = jnp.concatenate([d_query, d_key, d_values.reshape(ROWS, HID)], axis=1).astype(jnp.bfloat16)
    d_pre = (d_hidden * gelu_slope(pre_act)).astype(jnp.bfloat16)
    grad_normalized_rows = jnp.dot(d_joined, joined.T, preferred_element_type=jnp.float32)
    grad_normalized_rows = grad_normalized_rows + jnp.dot(d_pre, expand_weight.T, preferred_element_type=jnp.float32)
    block_input_gradient = (cotangent.astype(jnp.float32) + layer_norm_backward(grad_normalized_rows, centered_scaled_input, inverse_row_deviation)).astype(jnp.bfloat16)
    triple_grad = replica_sum(normed_rows, d_joined).reshape(MODEL_WIDTH, 3, HID)
    expand_grad = replica_sum(normed_rows, d_pre)
    merge_grad = replica_sum(cotangent, attended)
    shrink_grad = replica_sum(cotangent, hidden)
    return (outputs, block_input_gradient, triple_grad, expand_grad, merge_grad, shrink_grad)
```

```python
import functools
import math

import jax
import jax.numpy as jnp
from jax import lax
from jax.experimental import pallas as pl
from jax.experimental.pallas import tpu as pltpu
from jax.sharding import PartitionSpec as P

MESH = pl.DeviceIdType.MESH
F32 = jnp.float32
BF16 = jnp.bfloat16

WIDTH = 6144
EPS = 1e-06
ROOT_HALF = 0.7071067811865476
INV_ROOT_TAU = 0.3989422804014327
SCALE = 1.0 / math.sqrt(128)
VMEM_LIMIT = 56 * 1024 * 1024

SEQ = ((0, 1, 2), (1, 2, 0), (2, 0, 1))


def place():
    m = lax.axis_index("mx")
    c = m % 2
    y = (m // 2) % 4
    z = m // 8
    return lax.axis_index("dp"), m, lax.axis_index("my"), y, z, c


def partners(m, y, z, c):
    return (m + 2 * (1 - 2 * (y % 2)), m + 2 * (3 - 2 * y), m + 8 - 16 * z, m + 1 - 2 * c)


def owner_of(y, z, c, da, db, dz, dc):
    b = (y // 2 + db) % 2
    a = (y + y // 2 + da) % 2
    return 2 * b + (a + b) % 2, (z + dz) % 2, (c + dc) % 2


def slot_bits(p, t):
    d = (t // 4, (t // 2) % 2, t % 2)
    bits = [None, None, None]
    for place_at, axis in enumerate(SEQ[p]):
        bits[axis] = d[place_at]
    return bits


def share_columns(yo, zo, co):
    k = zo * 2 + co
    head = 3 * yo + k
    unit = 6 * yo + k
    usual = (("m", head), ("s", unit), ("t", head), ("t", 12 + head), ("t", 24 + head), ("e", unit))
    first = 6 * yo + 3
    fourth = (("s", first), ("s", first + 1), ("s", first + 2), ("e", first), ("e", first + 1), ("e", first + 2))
    return k == 3, usual, fourth


def lanes(index):
    return pl.ds(pl.multiple_of(index * 128, 128), 128)


def load_weights(p, refs, held, sem, y, z, c):
    def step(s, carry):
        yo, zo, co = owner_of(y, z, c, s // 8, (s // 4) % 2, (s // 2) % 2, s % 2)
        fourth, usual, last = share_columns(yo, zo, co)

        def start(blocks):
            for half in range(2):
                name, index = blocks[2 * p + half]
                pltpu.make_async_copy(
                    refs[name].at[:, lanes(index)], held.at[p, s, :, pl.ds(128 * half, 128)], sem.at[p]
                ).start()

        @pl.when(fourth)
        def _():
            start(last)

        @pl.when(jnp.logical_not(fourth))
        def _():
            start(usual)

        return carry

    lax.fori_loop(0, 16, step, 0)


def wait_weights(p, held, sem):
    pltpu.make_async_copy(held.at[p], held.at[p], sem.at[p]).wait()


def remote(src, dst, send, recv, device):
    return pltpu.make_async_remote_copy(
        src_ref=src, dst_ref=dst, send_sem=send, recv_sem=recv, device_id=device, device_id_type=MESH
    )


def greet(devices):
    barrier = pltpu.get_barrier_semaphore()
    for device in devices:
        pl.semaphore_signal(barrier, inc=1, device_id=device, device_id_type=MESH)
    pl.semaphore_wait(barrier, len(devices))


def dot_last(left, right):
    return lax.dot_general(left, right, (((1,), (1,)), ((), ())), preferred_element_type=F32)


def dot_first(left, right):
    return lax.dot_general(left, right, (((0,), (0,)), ((), ())), preferred_element_type=F32)


def project_kernel(
    inp, cot, tri, exp, mer, shr, out, nown, nfull, cfull, unit_out, inv_out,
    held, part, got0, got1, got2, got3, stat_out, stat_in, both,
    wsem, xs, xr, ss, sr, rs, rr,
):
    r, m, x, y, z, c = place()
    refs = {"t": tri, "e": exp, "m": mer, "s": shr}
    peers = partners(m, y, z, c)
    xpeers = [(x + i) % 4 for i in (1, 2, 3)]
    load_weights(0, refs, held, wsem, y, z, c)
    greet([{"my": q} for q in xpeers] + [{"mx": q} for q in peers])

    own = pl.ds(pl.multiple_of(x * 64, 64), 64)
    sends = []
    for i in range(3):
        copy = remote(cot, cfull.at[own], xs.at[0, i], xr.at[0, i], {"my": xpeers[i]})
        copy.start()
        sends.append(copy)
    cfull[own, :] = cot[...]

    rows = inp[...].astype(F32)
    mean = jnp.sum(rows, axis=1, keepdims=True) / rows.shape[1]
    centred = rows - mean
    square = jnp.sum(centred * centred, axis=1, keepdims=True)
    low = lax.broadcasted_iota(jnp.int32, (64, 128), 1) < 64
    count = float(rows.shape[1])
    for step in range(4):
        stat_out[step] = jnp.where(low, mean, square)
        copy = remote(
            stat_out.at[step], stat_in.at[step], ss.at[step], sr.at[step], {"mx": peers[(3, 0, 1, 2)[step]]}
        )
        copy.start()
        if step == 0:
            for p in (1, 2):
                load_weights(p, refs, held, wsem, y, z, c)
        copy.wait_recv()
        sends.append(copy)
        other = stat_in[step]
        mean2, square2 = other[:, 0:1], other[:, 64:65]
        delta = mean2 - mean
        square = square + square2 + delta * delta * (count / 2)
        mean = (mean + mean2) * 0.5
        count = count * 2
    inverse = lax.rsqrt(square / WIDTH + EPS)
    unit = (rows - mean) * inverse
    unit_out[...] = unit
    inv_out[...] = jnp.broadcast_to(inverse, (64, 128))
    nown[...] = unit.astype(BF16)
    nfull[own, :] = unit.astype(BF16)
    for i in range(3):
        copy = remote(nown, nfull.at[own], xs.at[1, i], xr.at[1, i], {"my": xpeers[i]})
        copy.start()
        sends.append(copy)

    def gathered(k, full):
        for i in range(3):
            rows_of = pl.ds(pl.multiple_of(((x + 3 - i) % 4) * 64, 64), 64)
            remote(full.at[rows_of], full.at[rows_of], xs.at[k, i], xr.at[k, i], {"my": xpeers[i]}).wait_recv()

    def multiply(p, dc):
        def step(t, carry):
            da, db, dz = slot_bits(p, t)
            s = da * 8 + db * 4 + dz * 2 + dc
            if p == 1:
                fourth = ((z + dz) % 2) * ((c + dc) % 2)
                first = jnp.dot(both[fourth], held[p, s, :, 0:128], preferred_element_type=F32)
                second = jnp.dot(both[0], held[p, s, :, 128:256], preferred_element_type=F32)
                part[p, dc, t, :, 0:128] = first.astype(BF16)
                part[p, dc, t, :, 128:256] = second.astype(BF16)
            else:
                full = both[1 if p == 0 else 0]
                part[p, dc, t] = jnp.dot(full, held[p, s], preferred_element_type=F32).astype(BF16)
            return carry

        lax.fori_loop(0, 8, step, 0)

    def stage(p, k):
        if k == 0:
            return remote(part.at[p, 1], got0.at[p], rs.at[p, 0], rr.at[p, 0], {"mx": peers[3]})
        size = 8 >> k
        target = (None, got1, got2, got3)[k]
        return remote(
            part.at[p, 0, pl.ds(size, size)], target.at[p], rs.at[p, k], rr.at[p, k],
            {"mx": peers[SEQ[p][k - 1]]},
        )

    def absorb(p, k):
        stage(p, k).wait_recv()
        source = (got0, got1, got2, got3)[k]

        def step(t, carry):
            part[p, 0, t] = (part[p, 0, t].astype(F32) + source[p, t].astype(F32)).astype(BF16)
            return carry

        if k < 3:
            lax.fori_loop(0, 8 >> k, step, 0)
        else:
            out[p] = part[p, 0, 0].astype(F32) + source[p, 0].astype(F32)

    gathered(0, cfull)
    both[1] = cfull[...]
    wait_weights(0, held, wsem)
    multiply(0, 1)
    stage(0, 0).start()
    multiply(0, 0)
    gathered(1, nfull)
    both[0] = nfull[...]
    wait_weights(1, held, wsem)
    multiply(1, 1)
    stage(1, 0).start()
    multiply(1, 0)
    absorb(0, 0)
    stage(0, 1).start()
    wait_weights(2, held, wsem)
    multiply(2, 1)
    stage(2, 0).start()
    multiply(2, 0)
    absorb(1, 0)
    stage(1, 1).start()
    absorb(2, 0)
    stage(2, 1).start()
    for k in (1, 2):
        for p in range(3):
            absorb(p, k)
            stage(p, k + 1).start()
    for p in range(3):
        absorb(p, 3)
    for copy in sends:
        copy.wait_send()
    for p in range(3):
        for k in range(4):
            stage(p, k).wait_send()


def norm_heads(block):
    centre = block - jnp.mean(block, axis=-1, keepdims=True)
    inverse = lax.rsqrt(jnp.mean(centre * centre, axis=-1, keepdims=True) + EPS)
    return centre * inverse, inverse


def norm_backward(grad, unit, inverse):
    first = jnp.mean(grad, axis=-1, keepdims=True)
    second = jnp.mean(grad * unit, axis=-1, keepdims=True)
    return (grad - first - unit * second) * inverse


def gelu_pair(pre):
    phi = 0.5 * (1.0 + lax.erf(pre * ROOT_HALF))
    return pre * phi, phi + pre * jnp.exp(-0.5 * pre * pre) * INV_ROOT_TAU


def middle_kernel(proj, out):
    r, m, x, y, z, c = place()
    fourth = z * 2 + c == 3

    def left(p):
        return (p, slice(None), slice(0, 128))

    def right(p):
        return (p, slice(None), slice(128, 256))

    def unit(pre_at, grad_at):
        value, slope = gelu_pair(proj[pre_at])
        grad = proj[grad_at]
        out[grad_at] = value.astype(BF16)
        out[pre_at] = (grad * slope).astype(BF16)

    @pl.when(fourth)
    def _():
        unit(right(1), left(0))
        unit(left(2), right(0))
        unit(right(2), left(1))

    @pl.when(jnp.logical_not(fourth))
    def _():
        unit(right(2), right(0))
        qhat, qinv = norm_heads(proj[left(1)])
        khat, kinv = norm_heads(proj[right(1)])
        q, k = qhat.astype(BF16), khat.astype(BF16)
        v = proj[left(2)].astype(BF16)
        datt = proj[left(0)].astype(BF16)
        expo = jnp.exp(dot_last(q, k) * SCALE)
        probs = expo / jnp.sum(expo, axis=-1, keepdims=True)
        half = probs.astype(BF16)
        out[left(0)] = jnp.dot(half, v, preferred_element_type=F32).astype(BF16)
        g = dot_last(datt, v)
        ds = (probs * (g - jnp.sum(probs * g, axis=-1, keepdims=True))).astype(BF16)
        dqn = jnp.dot(ds, k, preferred_element_type=F32) * SCALE
        dkn = dot_first(ds, q) * SCALE
        out[left(1)] = norm_backward(dqn, qhat, qinv).astype(BF16)
        out[right(1)] = norm_backward(dkn, khat, kinv).astype(BF16)
        out[left(2)] = dot_first(half, datt).astype(BF16)


def gather_kernel(
    down, inp, cot, unit, inv, tri, exp, mer, shr, outputs, block_grad, ring,
    held, slots, acc, xsend, xgot, stat_out, stat_in,
    wsem, zs, zr, ys, yr, cs, cr, xs, xr, ss, sr,
):
    r, m, x, y, z, c = place()
    refs = {"t": tri, "e": exp, "m": mer, "s": shr}
    peers = partners(m, y, z, c)
    xpeers = [(x + i) % 4 for i in (1, 2, 3)]
    inner = m % 8
    up = {"dp": (r + z) % 4, "mx": inner + 8 * (1 - z)}
    below = {"dp": (r + 3 + z) % 4, "mx": inner + 8 * (1 - z)}
    greet([up, below] + [{"mx": peers[q]} for q in (0, 1, 3)] + [{"my": q} for q in xpeers])

    top, bottom = pl.ds(0, 128), pl.ds(128, 128)

    def hop(k, way):
        sem = (zs.at[way, k], zr.at[way, k])
        if way == 0:
            src = down if k == 0 else ring.at[8 - k]
            dst = ring.at[7 - k]
            if k == 3:
                src, dst = src.at[:, top], dst.at[:, top]
            return remote(src, dst, *sem, up)
        src = down if k == 0 else ring.at[k]
        dst = ring.at[k + 1]
        if k == 3:
            src, dst = src.at[:, bottom], dst.at[:, bottom]
        return remote(src, dst, *sem, below)

    def y_send(dz, k):
        src = down if dz == 0 else ring.at[1 + 6 * z]
        sem = (ys.at[dz, k], yr.at[dz, k])
        if k == 0:
            return remote(src, slots.at[dz, 2, 0], *sem, {"mx": peers[0]})
        if k == 1:
            return remote(src, slots.at[dz, 1, 0], *sem, {"mx": peers[1]})
        if k == 2:
            return remote(slots.at[dz, 2, 0, :, top], slots.at[dz, 3, 0, :, top], *sem, {"mx": peers[1]})
        return remote(slots.at[dz, 1, 0, :, bottom], slots.at[dz, 3, 0, :, bottom], *sem, {"mx": peers[0]})

    def core_send(dz, ab):
        src = slots.at[dz, ab, 0]
        if ab == 0:
            src = down if dz == 0 else ring.at[1 + 6 * z]
        return remote(src, slots.at[dz, ab, 1], cs.at[dz, ab], cr.at[dz, ab], {"mx": peers[3]})

    hop(0, 0).start()
    hop(0, 1).start()
    y_send(0, 0).start()
    y_send(0, 1).start()
    core_send(0, 0).start()
    for p in range(3):
        load_weights(p, refs, held, wsem, y, z, c)
    ring[0] = down[...]
    acc[...] = jnp.zeros_like(acc)
    for p in range(3):
        wait_weights(p, held, wsem)

    def multiply(data, dz, ab, dc):
        s = ab * 4 + dz * 2 + dc
        fourth = ((z + dz) % 2) * ((c + dc) % 2)
        acc[0] += dot_last(data[0], held[0, s])
        acc[1] += dot_last(data[1, :, 128:256], held[1, s, :, 128:256]) + dot_last(data[2], held[2, s])
        acc[1 - fourth] += dot_last(data[1, :, 0:128], held[1, s, :, 0:128])

    def take(dz, ab):
        core_send(dz, ab).start()
        multiply(slots.at[dz, ab, 0], dz, ab, 0)

    def take_other(dz, ab):
        core_send(dz, ab).wait_recv()
        multiply(slots.at[dz, ab, 1], dz, ab, 1)

    multiply(down, 0, 0, 0)
    hop(0, 0).wait_recv()
    hop(0, 1).wait_recv()
    hop(1, 0).start()
    hop(1, 1).start()
    y_send(1, 0).start()
    y_send(1, 1).start()
    core_send(1, 0).start()
    y_send(0, 0).wait_recv()
    y_send(0, 2).start()
    y_send(0, 1).wait_recv()
    y_send(0, 3).start()
    take(0, 2)
    take(0, 1)
    multiply(ring.at[1 + 6 * z], 1, 0, 0)
    take_other(0, 0)
    hop(1, 0).wait_recv()
    hop(1, 1).wait_recv()
    hop(2, 0).start()
    hop(2, 1).start()
    take_other(1, 0)
    y_send(1, 0).wait_recv()
    y_send(1, 2).start()
    y_send(1, 1).wait_recv()
    y_send(1, 3).start()
    y_send(0, 2).wait_recv()
    y_send(0, 3).wait_recv()
    take(0, 3)
    take(1, 2)
    take(1, 1)
    hop(2, 0).wait_recv()
    hop(2, 1).wait_recv()
    hop(3, 0).start()
    hop(3, 1).start()
    for ab in (2, 1, 3):
        take_other(0, ab)
    y_send(1, 2).wait_recv()
    y_send(1, 3).wait_recv()
    take(1, 3)
    for ab in (2, 1, 3):
        take_other(1, ab)

    xsend[...] = acc[...].astype(BF16)

    def x_send(i):
        rows_of = pl.ds(pl.multiple_of(xpeers[i] * 64, 64), 64)
        return remote(xsend.at[:, rows_of], xgot.at[i], xs.at[i], xr.at[i], {"my": xpeers[i]})

    for i in range(3):
        x_send(i).start()
    own = pl.ds(pl.multiple_of(x * 64, 64), 64)
    branch = acc[0, own, :]
    grad = acc[1, own, :]
    for i in range(3):
        x_send(i).wait_recv()
        branch = branch + xgot[i, 0].astype(F32)
        grad = grad + xgot[i, 1].astype(F32)
    outputs[...] = (inp[...].astype(F32) + branch).astype(BF16)
    hat = unit[...]
    first = jnp.sum(grad, axis=1, keepdims=True)
    second = jnp.sum(grad * hat, axis=1, keepdims=True)
    low = lax.broadcasted_iota(jnp.int32, (64, 128), 1) < 64
    for step in range(4):
        stat_out[step] = jnp.where(low, first, second)
        copy = remote(
            stat_out.at[step], stat_in.at[step], ss.at[step], sr.at[step], {"mx": peers[(3, 0, 1, 2)[step]]}
        )
        copy.start()
        copy.wait()
        other = stat_in[step]
        first = first + other[:, 0:1]
        second = second + other[:, 64:65]
    fixed = (grad - first / WIDTH - hat * (second / WIDTH)) * inv[:, 0:1]
    block_grad[...] = (cot[...].astype(F32) + fixed).astype(BF16)

    hop(3, 0).wait_recv()
    hop(3, 1).wait_recv()
    for k in range(4):
        for way in range(2):
            hop(k, way).wait_send()
    for dz in range(2):
        for k in range(4):
            y_send(dz, k).wait_send()
            core_send(dz, k).wait_send()
    for i in range(3):
        x_send(i).wait_send()


def weight_kernel(ring, rows, tri, exp, mer, shr, left, res, got, lsem, osem, gs, gr):
    r, m, x, y, z, c = place()
    me = m % 8
    refs = {"t": tri, "e": exp, "m": mer, "s": shr}
    others = [(me + i) % 8 for i in range(1, 8)]
    for q in range(8):
        pltpu.make_async_copy(rows.at[q], left.at[:, :, pl.ds(96 * q, 96)], lsem).start()
    greet([{"mx": q + 8 * z} for q in others])
    pltpu.make_async_copy(left, left, lsem).wait()

    def result(dz, p, i):
        q = others[i]
        return remote(
            res.at[dz, p, q], got.at[dz, p, me], gs.at[dz, p, i], gr.at[dz, p, i], {"mx": q + 8 * z}
        )

    for dz in range(2):
        zo = (z + dz) % 2
        fourth = zo * c
        for p in range(3):
            def pick(k):
                d = (dz * (1 + 6 * z) + 2 * k) % 8
                return (r + (k if dz else k)) % 4, d

            def total(side, columns):
                acc = None
                for k in range(4):
                    rep, d = pick(k)
                    term = jnp.dot(left[side, rep], ring[d, p, :, columns], preferred_element_type=F32)
                    acc = term if acc is None else acc + term
                return acc.astype(BF16).reshape(8, 96, -1)

            if p == 1:
                res[dz, p, :, :, 0:128] = total(fourth, slice(0, 128))
                res[dz, p, :, :, 128:256] = total(0, slice(128, 256))
            else:
                res[dz, p] = total(1 if p == 0 else 0, slice(0, 256))
            got[dz, p, me] = res[dz, p, me]
            for i in range(7):
                result(dz, p, i).start()

    for dz in range(2):
        for p in range(3):
            for i in range(7):
                result(dz, p, i).wait_recv()

            def store(q, carry):
                fourth, usual, last = share_columns(q // 2, (z + dz) % 2, q % 2)

                def start(blocks):
                    for half in range(2):
                        name, index = blocks[2 * p + half]
                        pltpu.make_async_copy(
                            got.at[dz, p, q, :, pl.ds(128 * half, 128)], refs[name].at[:, lanes(index)], osem
                        ).start()

                @pl.when(fourth)
                def _():
                    start(last)

                @pl.when(jnp.logical_not(fourth))
                def _():
                    start(usual)

                return carry

            lax.fori_loop(0, 8, store, 0)
    for dz in range(2):
        for p in range(3):
            for i in range(7):
                result(dz, p, i).wait_send()
    pltpu.make_async_copy(got, got, osem).wait()


def params(number=None):
    if number is None:
        return pltpu.CompilerParams(vmem_limit_bytes=VMEM_LIMIT)
    return pltpu.CompilerParams(collective_id=number, has_side_effects=True, vmem_limit_bytes=VMEM_LIMIT)


VM = pl.BlockSpec(memory_space=pltpu.VMEM)
HB = pl.BlockSpec(memory_space=pl.ANY)
SEM = pltpu.SemaphoreType.DMA


def shape(*dims, dtype=BF16):
    return jax.ShapeDtypeStruct(dims, dtype)


def project(inp, cot, tri, exp, mer, shr):
    return pl.pallas_call(
        project_kernel,
        out_shape=(
            shape(3, 256, 256, dtype=F32), shape(64, 384), shape(256, 384), shape(256, 384),
            shape(64, 384, dtype=F32), shape(64, 128, dtype=F32),
        ),
        in_specs=[VM, VM, HB, HB, HB, HB],
        out_specs=(VM,) * 6,
        scratch_shapes=[
            pltpu.VMEM((3, 16, 384, 256), BF16),
            pltpu.VMEM((3, 2, 8, 256, 256), BF16),
            pltpu.VMEM((3, 8, 256, 256), BF16),
            pltpu.VMEM((3, 4, 256, 256), BF16),
            pltpu.VMEM((3, 2, 256, 256), BF16),
            pltpu.VMEM((3, 1, 256, 256), BF16),
            pltpu.VMEM((4, 64, 128), F32),
            pltpu.VMEM((4, 64, 128), F32),
            pltpu.VMEM((2, 256, 384), BF16),
            SEM((3,)), SEM((2, 3)), SEM((2, 3)), SEM((4,)), SEM((4,)), SEM((3, 4)), SEM((3, 4)),
        ],
        compiler_params=params(0),
        name="project",
    )(inp, cot, tri, exp, mer, shr)


def middle(proj):
    return pl.pallas_call(
        middle_kernel,
        out_shape=shape(3, 256, 256),
        in_specs=[VM],
        out_specs=VM,
        compiler_params=params(),
        name="middle",
    )(proj)


def gather(down, inp, cot, unit, inv, tri, exp, mer, shr):
    return pl.pallas_call(
        gather_kernel,
        out_shape=(shape(64, 384), shape(64, 384), shape(8, 3, 256, 256)),
        in_specs=[VM] * 5 + [HB] * 4,
        out_specs=(VM,) * 3,
        scratch_shapes=[
            pltpu.VMEM((3, 16, 384, 256), BF16),
            pltpu.VMEM((2, 4, 2, 3, 256, 256), BF16),
            pltpu.VMEM((2, 256, 384), F32),
            pltpu.VMEM((2, 256, 384), BF16),
            pltpu.VMEM((3, 2, 64, 384), BF16),
            pltpu.VMEM((4, 64, 128), F32),
            pltpu.VMEM((4, 64, 128), F32),
            SEM((3,)), SEM((2, 4)), SEM((2, 4)), SEM((2, 4)), SEM((2, 4)), SEM((2, 4)), SEM((2, 4)),
            SEM((3,)), SEM((3,)), SEM((4,)), SEM((4,)),
        ],
        compiler_params=params(1),
        name="gather",
    )(down, inp, cot, unit, inv, tri, exp, mer, shr)


def weight_grads(ring, rows):
    return pl.pallas_call(
        weight_kernel,
        out_shape=(shape(96, 4608), shape(96, 3072), shape(96, 1536), shape(96, 3072)),
        in_specs=[VM, HB],
        out_specs=(HB,) * 4,
        scratch_shapes=[
            pltpu.VMEM((2, 4, 768, 256), BF16),
            pltpu.VMEM((2, 3, 8, 96, 256), BF16),
            pltpu.VMEM((2, 3, 8, 96, 256), BF16),
            SEM(()), SEM(()), SEM((2, 3, 7)), SEM((2, 3, 7)),
        ],
        compiler_params=params(2),
        name="weights",
    )(ring, rows)


def row_shares(normed, cot):
    pair = jnp.stack([normed, cot])
    all_reps = lax.all_gather(pair, "dp")
    mine = lax.dynamic_slice_in_dim(all_reps, lax.axis_index("dp") * 96, 96, axis=3)
    turned = mine.transpose(1, 0, 3, 2)
    wide = lax.all_gather(turned, "my", axis=3, tiled=True)
    return lax.all_gather(wide, "mx", axis_index_groups=[list(range(8)), list(range(8, 16))])


def body(inputs, triple_weight, expand_weight, merge_weight, shrink_weight, cotangent):
    tri = triple_weight.reshape(triple_weight.shape[0], -1)
    weights = (tri, expand_weight, merge_weight, shrink_weight)
    proj, normed, nfull, cfull, unit, inv = project(inputs, cotangent, *weights)
    rows = row_shares(normed, cotangent)
    down = middle(proj)
    outputs, block_grad, ring = gather(down, inputs, cotangent, unit, inv, *weights)
    tg, eg, mg, sg = weight_grads(ring, rows)
    return outputs, block_grad, tg.reshape(96, 3, -1), eg, mg, sg


def solution(mesh):
    placed = (
        P(("dp", "my"), "mx"),
        P("mx", None, "my"),
        P("mx", "my"),
        P("mx", "my"),
        P("mx", "my"),
        P(("dp", "my"), "mx"),
    )
    return jax.shard_map(
        body,
        mesh=mesh,
        in_specs=placed,
        out_specs=(
            P(("dp", "my"), "mx"),
            P(("dp", "my"), "mx"),
            P(("mx", "dp"), None, "my"),
            P(("mx", "dp"), "my"),
            P(("mx", "dp"), "my"),
            P(("mx", "dp"), "my"),
        ),
        check_vma=False,
    )
```

```python
import functools
import math

import jax
import jax.numpy as jnp
from jax import lax
from jax.experimental import pallas as pl
from jax.experimental.pallas import tpu as pltpu
from jax.sharding import PartitionSpec as P

MESH = pl.DeviceIdType.MESH
F32 = jnp.float32
BF16 = jnp.bfloat16

WIDTH = 6144
EPS = 1e-06
ROOT_HALF = 0.7071067811865476
INV_ROOT_TAU = 0.3989422804014327
SCALE = 1.0 / math.sqrt(128)
VMEM_LIMIT = 56 * 1024 * 1024

SEQ = ((0, 1, 2), (1, 2, 0), (2, 0, 1))
CUTS = (((0, 96), (96, 80), (176, 80)), ((0, 80), (80, 96), (176, 80)), ((0, 80), (80, 80), (160, 96)))


def place():
    m = lax.axis_index("mx")
    c = m % 2
    y = (m // 2) % 4
    z = m // 8
    return lax.axis_index("dp"), m, lax.axis_index("my"), y, z, c


def partners(m, y, z, c):
    return (m + 2 * (1 - 2 * (y % 2)), m + 2 * (3 - 2 * y), m + 8 - 16 * z, m + 1 - 2 * c)


def owner_of(y, z, c, da, db, dz, dc):
    b = (y // 2 + db) % 2
    a = (y + y // 2 + da) % 2
    return 2 * b + (a + b) % 2, (z + dz) % 2, (c + dc) % 2


def share_columns(yo, zo, co):
    k = zo * 2 + co
    head = 3 * yo + k
    unit = 6 * yo + k
    usual = (("m", head), ("s", unit), ("q", head), ("k", head), ("v", head), ("e", unit))
    first = 6 * yo + 3
    fourth = (("s", first), ("s", first + 1), ("s", first + 2), ("e", first), ("e", first + 1), ("e", first + 2))
    return k == 3, usual, fourth


def named(tri, exp, mer, shr):
    return {"q": tri.at[0], "k": tri.at[1], "v": tri.at[2], "e": exp, "m": mer, "s": shr}


def lanes(index):
    return pl.ds(pl.multiple_of(index * 128, 128), 128)


def load_weights(p, refs, held, sem, y, z, c):
    def step(s, carry):
        yo, zo, co = owner_of(y, z, c, s // 8, (s // 4) % 2, (s // 2) % 2, s % 2)
        fourth, usual, last = share_columns(yo, zo, co)

        def start(blocks):
            for half in range(2):
                name, index = blocks[2 * p + half]
                pltpu.make_async_copy(
                    refs[name].at[:, lanes(index)], held.at[p, s, :, pl.ds(128 * half, 128)], sem.at[p]
                ).start()

        @pl.when(fourth)
        def _():
            start(last)

        @pl.when(jnp.logical_not(fourth))
        def _():
            start(usual)

        return carry

    lax.fori_loop(0, 16, step, 0)


def wait_weights(p, held, sem):
    pltpu.make_async_copy(held.at[p], held.at[p], sem.at[p]).wait()


def remote(src, dst, send, recv, device):
    return pltpu.make_async_remote_copy(
        src_ref=src, dst_ref=dst, send_sem=send, recv_sem=recv, device_id=device, device_id_type=MESH
    )


def greet(devices):
    barrier = pltpu.get_barrier_semaphore()
    for device in devices:
        pl.semaphore_signal(barrier, inc=1, device_id=device, device_id_type=MESH)
    pl.semaphore_wait(barrier, len(devices))


def dot_last(left, right):
    return lax.dot_general(left, right, (((1,), (1,)), ((), ())), preferred_element_type=F32)


def dot_first(left, right):
    return lax.dot_general(left, right, (((0,), (0,)), ((), ())), preferred_element_type=F32)


def project_kernel(
    inp, cot, tri, exp, mer, shr, out, unit_out, inv_out, spread,
    held, part, got0, got1, got2, got3, stat_out, stat_in, nown, both, turned, mixed,
    wsem, xs, xr, ss, sr, rs, rr, es, er, fs, fr,
):
    r, m, x, y, z, c = place()
    refs = named(tri, exp, mer, shr)
    peers = partners(m, y, z, c)
    xpeers = [(x + i) % 4 for i in (1, 2, 3)]
    rpeers = [(r + i) % 4 for i in (1, 2, 3)]
    greet([{"my": q} for q in xpeers] + [{"mx": q} for q in peers] + [{"dp": q} for q in rpeers])

    own = pl.ds(pl.multiple_of(x * 64, 64), 64)
    sends = []
    for i in range(3):
        copy = remote(cot, both.at[1, own], xs.at[0, i], xr.at[0, i], {"my": xpeers[i]})
        copy.start()
        sends.append(copy)
    both[1, own, :] = cot[...]

    rows = inp[...].astype(F32)
    mean = jnp.sum(rows, axis=1, keepdims=True) / rows.shape[1]
    centred = rows - mean
    square = jnp.sum(centred * centred, axis=1, keepdims=True)
    low = lax.broadcasted_iota(jnp.int32, (64, 128), 1) < 64
    stats = [mean, square, float(rows.shape[1])]

    def stat_copy(step):
        return remote(
            stat_out.at[step], stat_in.at[step], ss.at[step], sr.at[step], {"mx": peers[(3, 0, 1, 2)[step]]}
        )

    def stat_start(step):
        stat_out[step] = jnp.where(low, stats[0], stats[1])
        stat_copy(step).start()

    def stat_finish(step):
        stat_copy(step).wait_recv()
        other = stat_in[step]
        mean2, square2 = other[:, 0:1], other[:, 64:65]
        delta = mean2 - stats[0]
        stats[1] = stats[1] + square2 + delta * delta * (stats[2] / 2)
        stats[0] = (stats[0] + mean2) * 0.5
        stats[2] = stats[2] * 2

    stat_start(0)
    load_weights(0, refs, held, wsem, y, z, c)
    stat_finish(0)
    stat_start(1)

    def gathered(k):
        for i in range(3):
            rows_of = both.at[1 - k, pl.ds(pl.multiple_of(((x + 3 - i) % 4) * 64, 64), 64)]
            remote(rows_of, rows_of, xs.at[k, i], xr.at[k, i], {"my": xpeers[i]}).wait_recv()

    def multiply(p, dc):
        def step(t, carry):
            da, db, dz = t // 4, (t // 2) % 2, t % 2
            s = t * 2 + dc
            places = (t, 4 * db + 2 * dz + da, 4 * dz + 2 * da + db)

            def put(value, columns):
                for q in range(3):
                    at, size = CUTS[p][q]
                    part[p, q, dc, places[q], 0:size, columns] = value[at : at + size]

            if p == 1:
                fourth = ((z + dz) % 2) * ((c + dc) % 2)
                first = jnp.dot(both[fourth], held[p, s, :, 0:128], preferred_element_type=F32)
                second = jnp.dot(both[0], held[p, s, :, 128:256], preferred_element_type=F32)
                put(first.astype(BF16), slice(0, 128))
                put(second.astype(BF16), slice(128, 256))
            else:
                full = both[1 if p == 0 else 0]
                put(jnp.dot(full, held[p, s], preferred_element_type=F32).astype(BF16), slice(0, 256))
            return carry

        lax.fori_loop(0, 8, step, 0)

    def stage(p, q, k):
        size = CUTS[p][q][1]
        sem = (rs.at[p, q, k], rr.at[p, q, k])
        if k == 0:
            return remote(part.at[p, q, 1, :, 0:size], got0.at[p, q, :, 0:size], *sem, {"mx": peers[3]})
        slots = 8 >> k
        target = (None, got1, got2, got3)[k]
        return remote(
            part.at[p, q, 0, pl.ds(slots, slots), 0:size], target.at[p, q, :, 0:size], *sem,
            {"mx": peers[SEQ[q][k - 1]]},
        )

    def begin(p):
        for q in range(3):
            stage(p, q, 0).start()

    def advance(p, k):
        source = (got0, got1, got2, got3)[k]
        for q in range(3):
            at, size = CUTS[p][q]
            stage(p, q, k).wait_recv()

            def step(t, carry):
                total = part[p, q, 0, t, 0:size].astype(F32) + source[p, q, t, 0:size].astype(F32)
                part[p, q, 0, t, 0:size] = total.astype(BF16)
                return carry

            if k < 3:
                lax.fori_loop(0, 8 >> k, step, 0)
                stage(p, q, k + 1).start()
            else:
                out[p, at : at + size] = (
                    part[p, q, 0, 0, 0:size].astype(F32) + source[p, q, 0, 0:size].astype(F32)
                )

    gathered(0)
    wait_weights(0, held, wsem)
    multiply(0, 1)
    begin(0)
    stat_finish(1)
    stat_start(2)
    multiply(0, 0)
    stat_finish(2)
    stat_start(3)
    advance(0, 0)
    load_weights(1, refs, held, wsem, y, z, c)
    stat_finish(3)
    mean, square = stats[0], stats[1]
    inverse = lax.rsqrt(square / WIDTH + EPS)
    unit = (rows - mean) * inverse
    nown[...] = unit.astype(BF16)
    both[0, own, :] = unit.astype(BF16)
    for i in range(3):
        copy = remote(nown, both.at[0, own], xs.at[1, i], xr.at[1, i], {"my": xpeers[i]})
        copy.start()
        sends.append(copy)
    unit_out[...] = unit
    inv_out[...] = jnp.broadcast_to(inverse, (64, 128))
    load_weights(2, refs, held, wsem, y, z, c)
    advance(0, 1)
    gathered(1)
    wait_weights(1, held, wsem)
    multiply(1, 1)
    begin(1)
    multiply(1, 0)
    advance(1, 0)
    wait_weights(2, held, wsem)
    multiply(2, 1)
    begin(2)
    multiply(2, 0)
    advance(0, 2)
    advance(2, 0)

    quarter = both[x // 2, pl.ds(pl.multiple_of((x % 2) * 128, 128), 128), :]
    turned[...] = quarter.T.reshape(4, 96, 128)

    def swap(i):
        q = rpeers[i]
        return remote(turned.at[q], mixed.at[3 - i], es.at[i], er.at[i], {"dp": q})

    def pass_on(k):
        sem = (fs.at[k], fr.at[k])
        if k == 0:
            return remote(mixed, spread.at[:, 2], *sem, {"mx": peers[0]})
        if k == 1:
            return remote(mixed, spread.at[:, 1], *sem, {"mx": peers[1]})
        if k == 2:
            return remote(spread.at[0:2, 2], spread.at[0:2, 3], *sem, {"mx": peers[1]})
        return remote(spread.at[2:4, 1], spread.at[2:4, 3], *sem, {"mx": peers[0]})

    for i in range(3):
        swap(i).start()
    mixed[0] = turned[r]
    advance(1, 1)
    advance(2, 1)
    for i in range(3):
        swap(i).wait_recv()
    pass_on(0).start()
    pass_on(1).start()
    spread[:, 0] = mixed[...]
    advance(1, 2)
    advance(2, 2)
    pass_on(0).wait_recv()
    pass_on(2).start()
    pass_on(1).wait_recv()
    pass_on(3).start()
    for p in range(3):
        advance(p, 3)
    pass_on(2).wait_recv()
    pass_on(3).wait_recv()
    for copy in sends:
        copy.wait_send()
    for step in range(4):
        stat_copy(step).wait_send()
        pass_on(step).wait_send()
    for i in range(3):
        swap(i).wait_send()
    for p in range(3):
        for q in range(3):
            for k in range(4):
                stage(p, q, k).wait_send()


def norm_heads(block):
    centre = block - jnp.mean(block, axis=-1, keepdims=True)
    inverse = lax.rsqrt(jnp.mean(centre * centre, axis=-1, keepdims=True) + EPS)
    return centre * inverse, inverse


def norm_backward(grad, unit, inverse):
    first = jnp.mean(grad, axis=-1, keepdims=True)
    second = jnp.mean(grad * unit, axis=-1, keepdims=True)
    return (grad - first - unit * second) * inverse


def gelu_pair(pre):
    phi = 0.5 * (1.0 + lax.erf(pre * ROOT_HALF))
    return pre * phi, phi + pre * jnp.exp(-0.5 * pre * pre) * INV_ROOT_TAU


def middle_kernel(proj, out):
    r, m, x, y, z, c = place()
    fourth = z * 2 + c == 3

    def left(p):
        return (p, slice(None), slice(0, 128))

    def right(p):
        return (p, slice(None), slice(128, 256))

    def unit(pre_at, grad_at):
        value, slope = gelu_pair(proj[pre_at])
        grad = proj[grad_at]
        out[grad_at] = value.astype(BF16)
        out[pre_at] = (grad * slope).astype(BF16)

    @pl.when(fourth)
    def _():
        unit(right(1), left(0))
        unit(left(2), right(0))
        unit(right(2), left(1))

    @pl.when(jnp.logical_not(fourth))
    def _():
        unit(right(2), right(0))
        qhat, qinv = norm_heads(proj[left(1)])
        khat, kinv = norm_heads(proj[right(1)])
        q, k = qhat.astype(BF16), khat.astype(BF16)
        v = proj[left(2)].astype(BF16)
        datt = proj[left(0)].astype(BF16)
        expo = jnp.exp(dot_last(q, k) * SCALE)
        probs = expo / jnp.sum(expo, axis=-1, keepdims=True)
        half = probs.astype(BF16)
        out[left(0)] = jnp.dot(half, v, preferred_element_type=F32).astype(BF16)
        g = dot_last(datt, v)
        ds = (probs * (g - jnp.sum(probs * g, axis=-1, keepdims=True))).astype(BF16)
        dqn = jnp.dot(ds, k, preferred_element_type=F32) * SCALE
        dkn = dot_first(ds, q) * SCALE
        out[left(1)] = norm_backward(dqn, qhat, qinv).astype(BF16)
        out[right(1)] = norm_backward(dkn, khat, kinv).astype(BF16)
        out[left(2)] = dot_first(half, datt).astype(BF16)


def finish_kernel(
    down, inp, cot, unit, inv, spread, tri, exp, mer, shr, outputs, block_grad, tgrad, egrad, mgrad, sgrad,
    held, slots, acc, xsend, xgot, stat_out, stat_in, ring, left, res, got,
    wsem, zs, zr, ys, yr, cs, cr, xs, xr, ss, sr, ls, lr, gs, gr, osem,
):
    r, m, x, y, z, c = place()
    refs = named(tri, exp, mer, shr)
    grads = named(tgrad, egrad, mgrad, sgrad)
    peers = partners(m, y, z, c)
    xpeers = [(x + i) % 4 for i in (1, 2, 3)]
    inner = m % 8
    up = {"dp": (r + z) % 4, "mx": inner + 8 * (1 - z)}
    below = {"dp": (r + 3 + z) % 4, "mx": inner + 8 * (1 - z)}
    other_core = 1 - 2 * c
    opposite = (m + 4) % 8 + 8 * z
    near = (None, peers[1], peers[0], opposite)

    def mate(dc, ab):
        base = m if ab == 0 else near[ab]
        return {"mx": base + other_core if dc else base}

    mates = [(dc, ab) for ab in (3, 2, 1, 0) for dc in (0, 1) if dc or ab]
    greet([up, below] + [mate(dc, ab) for dc, ab in mates] + [{"my": q} for q in xpeers])

    top, bottom = pl.ds(0, 128), pl.ds(128, 128)

    def hop(p, k, way):
        sem = (zs.at[p, k, way], zr.at[p, k, way])
        if way == 0:
            src = down.at[p] if k == 0 else ring.at[8 - k, p]
            dst = ring.at[7 - k, p]
            if k == 3:
                src, dst = src.at[top], dst.at[top]
            return remote(src, dst, *sem, up)
        src = down.at[p] if k == 0 else ring.at[k, p]
        dst = ring.at[k + 1, p]
        if k == 3:
            src, dst = src.at[bottom], dst.at[bottom]
        return remote(src, dst, *sem, below)

    def hop_start(p, k):
        hop(p, k, 0).start()
        hop(p, k, 1).start()

    def hop_wait(p, k):
        hop(p, k, 0).wait_recv()
        hop(p, k, 1).wait_recv()

    def y_send(dz, k):
        src = down if dz == 0 else ring.at[1 + 6 * z]
        sem = (ys.at[dz, k], yr.at[dz, k])
        if k == 0:
            return remote(src, slots.at[dz, 2, 0], *sem, {"mx": peers[0]})
        if k == 1:
            return remote(src, slots.at[dz, 1, 0], *sem, {"mx": peers[1]})
        if k == 2:
            return remote(slots.at[dz, 2, 0, :, top], slots.at[dz, 3, 0, :, top], *sem, {"mx": peers[1]})
        return remote(slots.at[dz, 1, 0, :, bottom], slots.at[dz, 3, 0, :, bottom], *sem, {"mx": peers[0]})

    def core_send(dz, ab):
        src = slots.at[dz, ab, 0]
        if ab == 0:
            src = down if dz == 0 else ring.at[1 + 6 * z]
        return remote(src, slots.at[dz, ab, 1], cs.at[dz, ab], cr.at[dz, ab], {"mx": peers[3]})

    def left_at(q):
        return left.at[q // 2, 0, :, :, :, lanes(q % 2)]

    def left_send(i):
        return remote(spread, left_at(x), ls.at[i], lr.at[i], {"my": xpeers[i]})

    left_core = remote(left.at[:, 0], left.at[:, 1], ls.at[3], lr.at[3], {"mx": peers[3]})

    for p in range(3):
        hop_start(p, 0)
    y_send(0, 0).start()
    y_send(0, 1).start()
    core_send(0, 0).start()
    for i in range(3):
        left_send(i).start()
    for p in range(3):
        load_weights(p, refs, held, wsem, y, z, c)
    left[x // 2, 0, :, :, :, lanes(x % 2)] = spread[...]
    ring[0] = down[...]
    acc[...] = jnp.zeros_like(acc)

    def multiply(data, dz, ab, dc):
        s = ab * 4 + dz * 2 + dc
        fourth = ((z + dz) % 2) * ((c + dc) % 2)
        acc[0] += dot_last(data[0], held[0, s])
        acc[1] += dot_last(data[1, :, 128:256], held[1, s, :, 128:256]) + dot_last(data[2], held[2, s])
        acc[1 - fourth] += dot_last(data[1, :, 0:128], held[1, s, :, 0:128])

    def use(dz, ab):
        multiply(slots.at[dz, ab, 0], dz, ab, 0)

    def use_other(dz, ab):
        core_send(dz, ab).wait_recv()
        multiply(slots.at[dz, ab, 1], dz, ab, 1)

    def result(dz, p, dc, ab):
        return remote(
            res.at[dz, p, dc, ab], got.at[dz, p, dc, ab], gs.at[dz, p, dc, ab], gr.at[dz, p, dc, ab], mate(dc, ab)
        )

    def weight_part(dz, p):
        fourth = ((z + dz) % 2) * c

        def total(dc, side, columns):
            sum_of = None
            for k in range(4):
                d = (dz * (1 + 6 * z) + 2 * k) % 8
                term = jnp.dot(
                    left[side, dc, k].reshape(384, 256), ring[d, p, :, columns], preferred_element_type=F32
                )
                sum_of = term if sum_of is None else sum_of + term
            return sum_of.astype(BF16).reshape(4, 96, -1)

        for dc in range(2):
            if p == 1:
                res[dz, p, dc, :, :, 0:128] = total(dc, fourth, slice(0, 128))
                res[dz, p, dc, :, :, 128:256] = total(dc, 0, slice(128, 256))
            else:
                res[dz, p, dc] = total(dc, 1 if p == 0 else 0, slice(0, 256))
        got[dz, p, 0, 0] = res[dz, p, 0, 0]
        for dc, ab in mates:
            result(dz, p, dc, ab).start()

    def store_part(dz, p):
        for dc, ab in mates:
            result(dz, p, dc, ab).wait_recv()

        def step(w, carry):
            yo, zo, co = owner_of(y, z, c, (w // 2) % 2, w % 2, dz, w // 4)
            fourth, usual, last = share_columns(yo, zo, co)

            def start(blocks):
                for half in range(2):
                    name, index = blocks[2 * p + half]
                    pltpu.make_async_copy(
                        got.at[dz, p, w // 4, w % 4, :, pl.ds(128 * half, 128)], grads[name].at[:, lanes(index)], osem
                    ).start()

            @pl.when(fourth)
            def _():
                start(last)

            @pl.when(jnp.logical_not(fourth))
            def _():
                start(usual)

            return carry

        lax.fori_loop(0, 8, step, 0)

    def x_send(i):
        rows_of = pl.ds(pl.multiple_of(xpeers[i] * 64, 64), 64)
        return remote(xsend.at[:, rows_of], xgot.at[i], xs.at[i], xr.at[i], {"my": xpeers[i]})

    for p in range(3):
        wait_weights(p, held, wsem)
    multiply(down, 0, 0, 0)
    hop_wait(0, 0)
    hop_start(0, 1)
    hop_wait(1, 0)
    hop_start(1, 1)
    hop_wait(2, 0)
    y_send(1, 0).start()
    y_send(1, 1).start()
    core_send(1, 0).start()
    y_send(0, 0).wait_recv()
    y_send(0, 2).start()
    core_send(0, 2).start()
    y_send(0, 1).wait_recv()
    y_send(0, 3).start()
    core_send(0, 1).start()
    use_other(0, 0)
    multiply(ring.at[1 + 6 * z], 1, 0, 0)
    hop_wait(0, 1)
    hop_start(0, 2)
    hop_wait(1, 1)
    hop_start(1, 2)
    use(0, 2)
    use(0, 1)
    use_other(1, 0)
    hop_wait(0, 2)
    hop_start(0, 3)
    hop_wait(1, 2)
    hop_start(1, 3)
    hop_start(2, 1)
    y_send(0, 2).wait_recv()
    y_send(0, 3).wait_recv()
    core_send(0, 3).start()
    y_send(1, 0).wait_recv()
    y_send(1, 2).start()
    core_send(1, 2).start()
    y_send(1, 1).wait_recv()
    y_send(1, 3).start()
    core_send(1, 1).start()
    for i in range(3):
        rows_of = left_at((x + 3 - i) % 4)
        remote(spread, rows_of, ls.at[i], lr.at[i], {"my": xpeers[i]}).wait_recv()
    left_core.start()
    use(0, 3)
    use_other(0, 2)
    use_other(0, 1)
    hop_wait(2, 1)
    hop_start(2, 2)
    hop_wait(0, 3)
    left_core.wait_recv()
    weight_part(0, 0)
    weight_part(1, 0)
    hop_wait(1, 3)
    hop_wait(2, 2)
    hop_start(2, 3)
    weight_part(0, 1)
    weight_part(1, 1)
    y_send(1, 2).wait_recv()
    y_send(1, 3).wait_recv()
    core_send(1, 3).start()
    use(1, 2)
    use(1, 1)
    use(1, 3)
    use_other(0, 3)
    for ab in (2, 1, 3):
        use_other(1, ab)

    xsend[...] = acc[...].astype(BF16)
    for i in range(3):
        x_send(i).start()
    hop_wait(2, 3)
    weight_part(0, 2)
    weight_part(1, 2)
    own = pl.ds(pl.multiple_of(x * 64, 64), 64)
    branch = acc[0, own, :]
    grad = acc[1, own, :]
    for i in range(3):
        x_send(i).wait_recv()
        branch = branch + xgot[i, 0].astype(F32)
        grad = grad + xgot[i, 1].astype(F32)
    outputs[...] = (inp[...].astype(F32) + branch).astype(BF16)
    hat = unit[...]
    first = jnp.sum(grad, axis=1, keepdims=True)
    second = jnp.sum(grad * hat, axis=1, keepdims=True)
    low = lax.broadcasted_iota(jnp.int32, (64, 128), 1) < 64
    parts = [(dz, p) for p in range(3) for dz in range(2)]
    for step in range(4):
        stat_out[step] = jnp.where(low, first, second)
        copy = remote(
            stat_out.at[step], stat_in.at[step], ss.at[step], sr.at[step], {"mx": peers[(3, 0, 1, 2)[step]]}
        )
        copy.start()
        if step < 3:
            store_part(*parts[step])
        copy.wait()
        other = stat_in[step]
        first = first + other[:, 0:1]
        second = second + other[:, 64:65]
    fixed = (grad - first / WIDTH - hat * (second / WIDTH)) * inv[:, 0:1]
    block_grad[...] = (cot[...].astype(F32) + fixed).astype(BF16)
    for dz, p in parts[3:]:
        store_part(dz, p)

    for p in range(3):
        for k in range(4):
            for way in range(2):
                hop(p, k, way).wait_send()
    for dz in range(2):
        for k in range(4):
            y_send(dz, k).wait_send()
            core_send(dz, k).wait_send()
    for i in range(3):
        x_send(i).wait_send()
        left_send(i).wait_send()
    left_core.wait_send()
    for dz, p in parts:
        for dc, ab in mates:
            result(dz, p, dc, ab).wait_send()
    pltpu.make_async_copy(got, got, osem).wait()


def params(number=None):
    if number is None:
        return pltpu.CompilerParams(vmem_limit_bytes=VMEM_LIMIT)
    return pltpu.CompilerParams(collective_id=number, has_side_effects=True, vmem_limit_bytes=VMEM_LIMIT)


VM = pl.BlockSpec(memory_space=pltpu.VMEM)
HB = pl.BlockSpec(memory_space=pl.ANY)
SEM = pltpu.SemaphoreType.DMA


def shape(*dims, dtype=BF16):
    return jax.ShapeDtypeStruct(dims, dtype)


def project(inp, cot, tri, exp, mer, shr):
    return pl.pallas_call(
        project_kernel,
        out_shape=(
            shape(3, 256, 256, dtype=F32), shape(64, 384, dtype=F32), shape(64, 128, dtype=F32), shape(4, 4, 96, 128),
        ),
        in_specs=[VM, VM, HB, HB, HB, HB],
        out_specs=(VM,) * 4,
        scratch_shapes=[
            pltpu.VMEM((3, 16, 384, 256), BF16),
            pltpu.VMEM((3, 3, 2, 8, 96, 256), BF16),
            pltpu.VMEM((3, 3, 8, 96, 256), BF16),
            pltpu.VMEM((3, 3, 4, 96, 256), BF16),
            pltpu.VMEM((3, 3, 2, 96, 256), BF16),
            pltpu.VMEM((3, 3, 1, 96, 256), BF16),
            pltpu.VMEM((4, 64, 128), F32),
            pltpu.VMEM((4, 64, 128), F32),
            pltpu.VMEM((64, 384), BF16),
            pltpu.VMEM((2, 256, 384), BF16),
            pltpu.VMEM((4, 96, 128), BF16),
            pltpu.VMEM((4, 96, 128), BF16),
            SEM((3,)), SEM((2, 3)), SEM((2, 3)), SEM((4,)), SEM((4,)), SEM((3, 3, 4)), SEM((3, 3, 4)),
            SEM((3,)), SEM((3,)), SEM((4,)), SEM((4,)),
        ],
        compiler_params=params(0),
        name="project",
    )(inp, cot, tri, exp, mer, shr)


def middle(proj):
    return pl.pallas_call(
        middle_kernel,
        out_shape=shape(3, 256, 256),
        in_specs=[VM],
        out_specs=VM,
        compiler_params=params(),
        name="middle",
    )(proj)


def finish(down, inp, cot, unit, inv, spread, tri, exp, mer, shr):
    return pl.pallas_call(
        finish_kernel,
        out_shape=(
            shape(64, 384), shape(64, 384), shape(3, 96, 1536), shape(96, 3072), shape(96, 1536), shape(96, 3072),
        ),
        in_specs=[VM] * 6 + [HB] * 4,
        out_specs=(VM, VM) + (HB,) * 4,
        scratch_shapes=[
            pltpu.VMEM((3, 16, 384, 256), BF16),
            pltpu.VMEM((2, 4, 2, 3, 256, 256), BF16),
            pltpu.VMEM((2, 256, 384), F32),
            pltpu.VMEM((2, 256, 384), BF16),
            pltpu.VMEM((3, 2, 64, 384), BF16),
            pltpu.VMEM((4, 64, 128), F32),
            pltpu.VMEM((4, 64, 128), F32),
            pltpu.VMEM((8, 3, 256, 256), BF16),
            pltpu.VMEM((2, 2, 4, 4, 96, 256), BF16),
            pltpu.VMEM((2, 3, 2, 4, 96, 256), BF16),
            pltpu.VMEM((2, 3, 2, 4, 96, 256), BF16),
            SEM((3,)), SEM((3, 4, 2)), SEM((3, 4, 2)), SEM((2, 4)), SEM((2, 4)), SEM((2, 4)), SEM((2, 4)),
            SEM((3,)), SEM((3,)), SEM((4,)), SEM((4,)), SEM((4,)), SEM((4,)),
            SEM((2, 3, 2, 4)), SEM((2, 3, 2, 4)), SEM(()),
        ],
        compiler_params=params(1),
        name="finish",
    )(down, inp, cot, unit, inv, spread, tri, exp, mer, shr)


def body(inputs, triple_weight, expand_weight, merge_weight, shrink_weight, cotangent):
    weights = (triple_weight.transpose(1, 0, 2), expand_weight, merge_weight, shrink_weight)
    proj, unit, inv, spread = project(inputs, cotangent, *weights)
    down = middle(proj)
    outputs, block_grad, tg, eg, mg, sg = finish(down, inputs, cotangent, unit, inv, spread, *weights)
    return outputs, block_grad, tg.transpose(1, 0, 2), eg, mg, sg


def solution(mesh):
    placed = (
        P(("dp", "my"), "mx"),
        P("mx", None, "my"),
        P("mx", "my"),
        P("mx", "my"),
        P("mx", "my"),
        P(("dp", "my"), "mx"),
    )
    return jax.shard_map(
        body,
        mesh=mesh,
        in_specs=placed,
        out_specs=(
            P(("dp", "my"), "mx"),
            P(("dp", "my"), "mx"),
            P(("mx", "dp"), None, "my"),
            P(("mx", "dp"), "my"),
            P(("mx", "dp"), "my"),
            P(("mx", "dp"), "my"),
        ),
        check_vma=False,
    )
```

```python
import math

import jax
import jax.numpy as jnp
from jax import lax
from jax.experimental import pallas as pl
from jax.experimental.pallas import tpu as pltpu
from jax.sharding import PartitionSpec as P

MESH = pl.DeviceIdType.MESH
F32 = jnp.float32
BF16 = jnp.bfloat16

WIDTH = 6144
EPS = 1e-06
ROOT_HALF = 0.7071067811865476
INV_ROOT_TAU = 0.3989422804014327
SCALE = 1.0 / math.sqrt(128)
VMEM_LIMIT = 60 * 1024 * 1024

SEQ = ((0, 1, 2), (1, 2, 0), (2, 0, 1))
CUTS = (((0, 96), (96, 80), (176, 80)), ((0, 80), (80, 96), (176, 80)), ((0, 80), (80, 80), (160, 96)))


def place():
    m = lax.axis_index("mx")
    c = m % 2
    y = (m // 2) % 4
    z = m // 8
    return lax.axis_index("dp"), m, lax.axis_index("my"), y, z, c


def partners(m, y, z, c):
    return (m + 2 * (1 - 2 * (y % 2)), m + 2 * (3 - 2 * y), m + 8 - 16 * z, m + 1 - 2 * c)


def owner_of(y, z, c, da, db, dz, dc):
    b = (y // 2 + db) % 2
    a = (y + y // 2 + da) % 2
    return 2 * b + (a + b) % 2, (z + dz) % 2, (c + dc) % 2


def share_columns(yo, zo, co):
    k = zo * 2 + co
    head = 3 * yo + k
    unit = 6 * yo + k
    usual = (("m", head), ("s", unit), ("q", head), ("k", head), ("v", head), ("e", unit))
    first = 6 * yo + 3
    fourth = (("s", first), ("s", first + 1), ("s", first + 2), ("e", first), ("e", first + 1), ("e", first + 2))
    return k == 3, usual, fourth


def named(tri, exp, mer, shr):
    return {"q": tri.at[0], "k": tri.at[1], "v": tri.at[2], "e": exp, "m": mer, "s": shr}


def lanes(index):
    return pl.ds(pl.multiple_of(index * 128, 128), 128)


def load_weights(p, refs, held, sem, y, z, c):
    def step(s, carry):
        yo, zo, co = owner_of(y, z, c, s // 8, (s // 4) % 2, (s // 2) % 2, s % 2)
        fourth, usual, last = share_columns(yo, zo, co)

        def start(blocks):
            for half in range(2):
                name, index = blocks[2 * p + half]
                pltpu.make_async_copy(
                    refs[name].at[:, lanes(index)], held.at[p, s, :, pl.ds(128 * half, 128)], sem.at[p]
                ).start()

        @pl.when(fourth)
        def _():
            start(last)

        @pl.when(jnp.logical_not(fourth))
        def _():
            start(usual)

        return carry

    lax.fori_loop(0, 16, step, 0)


def wait_weights(p, held, sem):
    pltpu.make_async_copy(held.at[p], held.at[p], sem.at[p]).wait()


def remote(src, dst, send, recv, device):
    return pltpu.make_async_remote_copy(
        src_ref=src, dst_ref=dst, send_sem=send, recv_sem=recv, device_id=device, device_id_type=MESH
    )


def greet(devices):
    barrier = pltpu.get_barrier_semaphore()
    for device in devices:
        pl.semaphore_signal(barrier, inc=1, device_id=device, device_id_type=MESH)
    pl.semaphore_wait(barrier, len(devices))


def dot_last(left, right):
    return lax.dot_general(left, right, (((1,), (1,)), ((), ())), preferred_element_type=F32)


def dot_first(left, right):
    return lax.dot_general(left, right, (((0,), (0,)), ((), ())), preferred_element_type=F32)


def norm_heads(block):
    centre = block - jnp.mean(block, axis=-1, keepdims=True)
    inverse = lax.rsqrt(jnp.mean(centre * centre, axis=-1, keepdims=True) + EPS)
    return centre * inverse, inverse


def norm_backward(grad, unit, inverse):
    first = jnp.mean(grad, axis=-1, keepdims=True)
    second = jnp.mean(grad * unit, axis=-1, keepdims=True)
    return (grad - first - unit * second) * inverse


def gelu_pair(pre):
    phi = 0.5 * (1.0 + lax.erf(pre * ROOT_HALF))
    return pre * phi, phi + pre * jnp.exp(-0.5 * pre * pre) * INV_ROOT_TAU


def middle(proj, out, fourth):
    def left(p):
        return (p, slice(None), slice(0, 128))

    def right(p):
        return (p, slice(None), slice(128, 256))

    def unit(pre_at, grad_at):
        value, slope = gelu_pair(proj[pre_at])
        grad = proj[grad_at]
        out[grad_at] = value.astype(BF16)
        out[pre_at] = (grad * slope).astype(BF16)

    @pl.when(fourth)
    def _():
        unit(right(1), left(0))
        unit(left(2), right(0))
        unit(right(2), left(1))

    @pl.when(jnp.logical_not(fourth))
    def _():
        unit(right(2), right(0))
        qhat, qinv = norm_heads(proj[left(1)])
        khat, kinv = norm_heads(proj[right(1)])
        q, k = qhat.astype(BF16), khat.astype(BF16)
        v = proj[left(2)].astype(BF16)
        datt = proj[left(0)].astype(BF16)
        expo = jnp.exp(dot_last(q, k) * SCALE)
        probs = expo / jnp.sum(expo, axis=-1, keepdims=True)
        half = probs.astype(BF16)
        out[left(0)] = jnp.dot(half, v, preferred_element_type=F32).astype(BF16)
        g = dot_last(datt, v)
        ds = (probs * (g - jnp.sum(probs * g, axis=-1, keepdims=True))).astype(BF16)
        dqn = jnp.dot(ds, k, preferred_element_type=F32) * SCALE
        dkn = dot_first(ds, q) * SCALE
        out[left(1)] = norm_backward(dqn, qhat, qinv).astype(BF16)
        out[right(1)] = norm_backward(dkn, khat, kinv).astype(BF16)
        out[left(2)] = dot_first(half, datt).astype(BF16)


def block_kernel(
    inp, cot, tri, exp, mer, shr, outputs, block_grad, got,
    held, part, got0, got1, got2, got3, stat_out, stat_in, nown, both, turned, mixed, spread, hat, proj, down,
    slots, acc, xsend, xgot, ring, left, res,
    wsem, xs, xr, ss, sr, rs, rr, es, er, fs, fr, zs, zr, ys, yr, cs, cr, ls, lr, gs, gr, osem,
):
    r, m, x, y, z, c = place()
    refs = named(tri, exp, mer, shr)
    peers = partners(m, y, z, c)
    xpeers = [(x + i) % 4 for i in (1, 2, 3)]
    rpeers = [(r + i) % 4 for i in (1, 2, 3)]
    inner = m % 8
    up = {"dp": (r + z) % 4, "mx": inner + 8 * (1 - z)}
    below = {"dp": (r + 3 + z) % 4, "mx": inner + 8 * (1 - z)}
    other_core = 1 - 2 * c
    opposite = (m + 4) % 8 + 8 * z
    near = (None, peers[1], peers[0], opposite)

    def mate(dc, ab):
        base = m if ab == 0 else near[ab]
        return {"mx": base + other_core if dc else base}

    mates = [(dc, ab) for ab in (3, 2, 1, 0) for dc in (0, 1) if dc or ab]
    rounds = (
        ({"mx": peers[3]}, {"mx": peers[2]}, {"mx": peers[2] + other_core}),
        ({"mx": peers[0]}, {"mx": peers[1]}, {"mx": opposite}),
    )
    greet(
        [{"my": q} for q in xpeers] + [{"dp": q} for q in rpeers] + [up, below, rounds[0][2]]
        + [mate(dc, ab) for dc, ab in mates]
    )

    own = pl.ds(pl.multiple_of(x * 64, 64), 64)
    sends = []
    for i in range(3):
        copy = remote(cot, both.at[1, own], xs.at[0, i], xr.at[0, i], {"my": xpeers[i]})
        copy.start()
        sends.append(copy)
    both[1, own, :] = cot[...]

    rows = inp[...].astype(F32)
    mean = jnp.sum(rows, axis=1, keepdims=True) / rows.shape[1]
    centred = rows - mean
    square = jnp.sum(centred * centred, axis=1, keepdims=True)
    low = lax.broadcasted_iota(jnp.int32, (64, 128), 1) < 64

    def stat_copy(k, i):
        return remote(stat_out.at[k], stat_in.at[k, i], ss.at[k, i], sr.at[k, i], rounds[k % 2][i])

    def stat_start(k, pair):
        stat_out[k] = jnp.where(low, pair[0], pair[1])
        for i in range(3):
            stat_copy(k, i).start()

    def stat_finish(k):
        pairs = []
        for i in range(3):
            stat_copy(k, i).wait_recv()
            pairs.append((stat_in[k, i, :, 0:1], stat_in[k, i, :, 64:65]))
        return pairs

    def combine(own_pair, pairs, count):
        pairs = [own_pair] + pairs
        middle_of = sum(pair[0] for pair in pairs) / 4
        spread_of = sum(pair[1] + count * (pair[0] - middle_of) ** 2 for pair in pairs)
        return middle_of, spread_of

    pair = (mean, square)
    stat_start(0, pair)
    load_weights(0, refs, held, wsem, y, z, c)
    pair = combine(pair, stat_finish(0), 384.0)
    stat_start(1, pair)

    def gathered(k):
        for i in range(3):
            rows_of = both.at[1 - k, pl.ds(pl.multiple_of(((x + 3 - i) % 4) * 64, 64), 64)]
            remote(rows_of, rows_of, xs.at[k, i], xr.at[k, i], {"my": xpeers[i]}).wait_recv()

    def multiply(p, dc):
        def step(t, carry):
            da, db, dz = t // 4, (t // 2) % 2, t % 2
            s = t * 2 + dc
            places = (t, 4 * db + 2 * dz + da, 4 * dz + 2 * da + db)

            def put(value, columns):
                for q in range(3):
                    at, size = CUTS[p][q]
                    part[p, q, dc, places[q], 0:size, columns] = value[at : at + size]

            if p == 1:
                fourth = ((z + dz) % 2) * ((c + dc) % 2)
                first = jnp.dot(both[fourth], held[p, s, :, 0:128], preferred_element_type=F32)
                second = jnp.dot(both[0], held[p, s, :, 128:256], preferred_element_type=F32)
                put(first.astype(BF16), slice(0, 128))
                put(second.astype(BF16), slice(128, 256))
            else:
                full = both[1 if p == 0 else 0]
                put(jnp.dot(full, held[p, s], preferred_element_type=F32).astype(BF16), slice(0, 256))
            return carry

        lax.fori_loop(0, 8, step, 0)

    def stage(p, q, k):
        size = CUTS[p][q][1]
        sem = (rs.at[p, q, k], rr.at[p, q, k])
        if k == 0:
            return remote(part.at[p, q, 1, :, 0:size], got0.at[p, q, :, 0:size], *sem, {"mx": peers[3]})
        slots = 8 >> k
        target = (None, got1, got2, got3)[k]
        return remote(
            part.at[p, q, 0, pl.ds(slots, slots), 0:size], target.at[p, q, :, 0:size], *sem,
            {"mx": peers[SEQ[q][k - 1]]},
        )

    def begin(p):
        for q in range(3):
            stage(p, q, 0).start()

    def advance(p, k):
        source = (got0, got1, got2, got3)[k]
        for q in range(3):
            at, size = CUTS[p][q]
            stage(p, q, k).wait_recv()

            def step(t, carry):
                total = part[p, q, 0, t, 0:size].astype(F32) + source[p, q, t, 0:size].astype(F32)
                part[p, q, 0, t, 0:size] = total.astype(BF16)
                return carry

            if k < 3:
                lax.fori_loop(0, 8 >> k, step, 0)
                stage(p, q, k + 1).start()
            else:
                proj[p, at : at + size] = (
                    part[p, q, 0, 0, 0:size].astype(F32) + source[p, q, 0, 0:size].astype(F32)
                )

    def swap(i):
        q = rpeers[i]
        return remote(turned.at[q], mixed.at[3 - i], es.at[i], er.at[i], {"dp": q})

    def pass_on(k):
        sem = (fs.at[k], fr.at[k])
        if k == 0:
            return remote(mixed, spread.at[:, 2], *sem, {"mx": peers[0]})
        if k == 1:
            return remote(mixed, spread.at[:, 1], *sem, {"mx": peers[1]})
        if k == 2:
            return remote(spread.at[0:2, 2], spread.at[0:2, 3], *sem, {"mx": peers[1]})
        return remote(spread.at[2:4, 1], spread.at[2:4, 3], *sem, {"mx": peers[0]})

    gathered(0)
    wait_weights(0, held, wsem)
    multiply(0, 1)
    begin(0)
    pair = combine(pair, stat_finish(1), 1536.0)
    inverse = lax.rsqrt(pair[1] / WIDTH + EPS)
    unit = (rows - pair[0]) * inverse
    nown[...] = unit.astype(BF16)
    both[0, own, :] = unit.astype(BF16)
    for i in range(3):
        copy = remote(nown, both.at[0, own], xs.at[1, i], xr.at[1, i], {"my": xpeers[i]})
        copy.start()
        sends.append(copy)
    hat[...] = unit
    multiply(0, 0)
    load_weights(1, refs, held, wsem, y, z, c)
    advance(0, 0)
    load_weights(2, refs, held, wsem, y, z, c)
    advance(0, 1)
    gathered(1)
    wait_weights(1, held, wsem)
    multiply(1, 1)
    begin(1)
    multiply(1, 0)
    wait_weights(2, held, wsem)
    multiply(2, 1)
    begin(2)
    advance(1, 0)

    quarter = both[x // 2, pl.ds(pl.multiple_of((x % 2) * 128, 128), 128), :]
    turned[...] = quarter.T.reshape(4, 96, 128)
    for i in range(3):
        swap(i).start()
    mixed[0] = turned[r]
    multiply(2, 0)
    advance(2, 0)
    advance(0, 2)
    advance(1, 1)
    advance(2, 1)
    for i in range(3):
        swap(i).wait_recv()
    pass_on(0).start()
    pass_on(1).start()
    spread[:, 0] = mixed[...]
    advance(1, 2)
    advance(2, 2)
    pass_on(0).wait_recv()
    pass_on(2).start()
    pass_on(1).wait_recv()
    pass_on(3).start()
    for p in range(3):
        advance(p, 3)
    middle(proj, down, z * 2 + c == 3)

    top, bottom = pl.ds(0, 128), pl.ds(128, 128)

    def hop(p, k, way):
        sem = (zs.at[p, k, way], zr.at[p, k, way])
        if way == 0:
            src = down.at[p] if k == 0 else ring.at[8 - k, p]
            dst = ring.at[7 - k, p]
            if k == 3:
                src, dst = src.at[top], dst.at[top]
            return remote(src, dst, *sem, up)
        src = down.at[p] if k == 0 else ring.at[k, p]
        dst = ring.at[k + 1, p]
        if k == 3:
            src, dst = src.at[bottom], dst.at[bottom]
        return remote(src, dst, *sem, below)

    def hop_start(p, k):
        hop(p, k, 0).start()
        hop(p, k, 1).start()

    def hop_wait(p, k):
        hop(p, k, 0).wait_recv()
        hop(p, k, 1).wait_recv()

    def y_send(dz, k):
        src = down if dz == 0 else ring.at[1 + 6 * z]
        sem = (ys.at[dz, k], yr.at[dz, k])
        if k == 0:
            return remote(src, slots.at[dz, 2, 0], *sem, {"mx": peers[0]})
        if k == 1:
            return remote(src, slots.at[dz, 1, 0], *sem, {"mx": peers[1]})
        if k == 2:
            return remote(slots.at[dz, 2, 0, :, top], slots.at[dz, 3, 0, :, top], *sem, {"mx": peers[1]})
        return remote(slots.at[dz, 1, 0, :, bottom], slots.at[dz, 3, 0, :, bottom], *sem, {"mx": peers[0]})

    def core_send(dz, ab):
        src = slots.at[dz, ab, 0]
        if ab == 0:
            src = down if dz == 0 else ring.at[1 + 6 * z]
        return remote(src, slots.at[dz, ab, 1], cs.at[dz, ab], cr.at[dz, ab], {"mx": peers[3]})

    def left_at(q):
        return left.at[q // 2, 0, :, :, :, lanes(q % 2)]

    def left_send(i):
        return remote(spread, left_at(x), ls.at[i], lr.at[i], {"my": xpeers[i]})

    left_core = remote(left.at[:, 0], left.at[:, 1], ls.at[3], lr.at[3], {"mx": peers[3]})

    for p in range(3):
        hop_start(p, 0)
    y_send(0, 0).start()
    y_send(0, 1).start()
    core_send(0, 0).start()
    pass_on(2).wait_recv()
    pass_on(3).wait_recv()
    for i in range(3):
        left_send(i).start()
    left[x // 2, 0, :, :, :, lanes(x % 2)] = spread[...]
    ring[0] = down[...]
    acc[...] = jnp.zeros_like(acc)

    def dgrad(data, dz, ab, dc):
        s = ab * 4 + dz * 2 + dc
        fourth = ((z + dz) % 2) * ((c + dc) % 2)
        acc[0] += dot_last(data[0], held[0, s])
        acc[1] += dot_last(data[1, :, 128:256], held[1, s, :, 128:256]) + dot_last(data[2], held[2, s])
        acc[1 - fourth] += dot_last(data[1, :, 0:128], held[1, s, :, 0:128])

    def use(dz, ab):
        dgrad(slots.at[dz, ab, 0], dz, ab, 0)

    def use_other(dz, ab):
        core_send(dz, ab).wait_recv()
        dgrad(slots.at[dz, ab, 1], dz, ab, 1)

    def result(dz, p, dc, ab):
        return remote(
            res.at[dz, p, dc, ab], got.at[dz, p, dc, ab], gs.at[dz, p, dc, ab], gr.at[dz, p, dc, ab], mate(dc, ab)
        )

    def weight_part(dz, p):
        fourth = ((z + dz) % 2) * c

        def total(dc, side, columns):
            sum_of = None
            for k in range(4):
                d = (dz * (1 + 6 * z) + 2 * k) % 8
                term = jnp.dot(
                    left[side, dc, k].reshape(384, 256), ring[d, p, :, columns], preferred_element_type=F32
                )
                sum_of = term if sum_of is None else sum_of + term
            return sum_of.astype(BF16).reshape(4, 96, -1)

        for dc in range(2):
            if p == 1:
                res[dz, p, dc, :, :, 0:128] = total(dc, fourth, slice(0, 128))
                res[dz, p, dc, :, :, 128:256] = total(dc, 0, slice(128, 256))
            else:
                res[dz, p, dc] = total(dc, 1 if p == 0 else 0, slice(0, 256))
        pltpu.make_async_copy(res.at[dz, p, 0, 0], got.at[dz, p, 0, 0], osem).start()
        for dc, ab in mates:
            result(dz, p, dc, ab).start()

    def x_send(i):
        rows_of = pl.ds(pl.multiple_of(xpeers[i] * 64, 64), 64)
        return remote(xsend.at[:, rows_of], xgot.at[i], xs.at[2, i], xr.at[2, i], {"my": xpeers[i]})

    dgrad(down, 0, 0, 0)
    hop_wait(0, 0)
    hop_start(0, 1)
    hop_wait(1, 0)
    hop_start(1, 1)
    hop_wait(2, 0)
    y_send(1, 0).start()
    y_send(1, 1).start()
    core_send(1, 0).start()
    y_send(0, 0).wait_recv()
    y_send(0, 2).start()
    core_send(0, 2).start()
    y_send(0, 1).wait_recv()
    y_send(0, 3).start()
    core_send(0, 1).start()
    use_other(0, 0)
    dgrad(ring.at[1 + 6 * z], 1, 0, 0)
    hop_wait(0, 1)
    hop_start(0, 2)
    hop_wait(1, 1)
    hop_start(1, 2)
    use(0, 2)
    use(0, 1)
    use_other(1, 0)
    hop_wait(0, 2)
    hop_start(0, 3)
    hop_wait(1, 2)
    hop_start(1, 3)
    hop_start(2, 1)
    y_send(0, 2).wait_recv()
    y_send(0, 3).wait_recv()
    core_send(0, 3).start()
    y_send(1, 0).wait_recv()
    y_send(1, 2).start()
    core_send(1, 2).start()
    y_send(1, 1).wait_recv()
    y_send(1, 3).start()
    core_send(1, 1).start()
    for i in range(3):
        rows_of = left_at((x + 3 - i) % 4)
        remote(spread, rows_of, ls.at[i], lr.at[i], {"my": xpeers[i]}).wait_recv()
    left_core.start()
    use(0, 3)
    use_other(0, 2)
    use_other(0, 1)
    hop_wait(2, 1)
    hop_start(2, 2)
    hop_wait(0, 3)
    left_core.wait_recv()
    weight_part(0, 0)
    weight_part(1, 0)
    hop_wait(1, 3)
    hop_wait(2, 2)
    hop_start(2, 3)
    weight_part(0, 1)
    weight_part(1, 1)
    y_send(1, 2).wait_recv()
    y_send(1, 3).wait_recv()
    core_send(1, 3).start()
    use(1, 2)
    use(1, 1)
    use(1, 3)
    use_other(0, 3)
    for ab in (2, 1, 3):
        use_other(1, ab)

    xsend[...] = acc[...].astype(BF16)
    for i in range(3):
        x_send(i).start()
    hop_wait(2, 3)
    weight_part(0, 2)
    weight_part(1, 2)
    own = pl.ds(pl.multiple_of(x * 64, 64), 64)
    branch = acc[0, own, :]
    grad = acc[1, own, :]
    for i in range(3):
        x_send(i).wait_recv()
        branch = branch + xgot[i, 0].astype(F32)
        grad = grad + xgot[i, 1].astype(F32)
    outputs[...] = (inp[...].astype(F32) + branch).astype(BF16)
    unit = hat[...]
    sums = (jnp.sum(grad, axis=1, keepdims=True), jnp.sum(grad * unit, axis=1, keepdims=True))
    for k in (2, 3):
        stat_start(k, sums)
        for pair in stat_finish(k):
            sums = (sums[0] + pair[0], sums[1] + pair[1])
    fixed = (grad - sums[0] / WIDTH - unit * (sums[1] / WIDTH)) * inverse
    block_grad[...] = (cot[...].astype(F32) + fixed).astype(BF16)

    parts = [(dz, p) for p in range(3) for dz in range(2)]
    for dz, p in parts:
        for dc, ab in mates:
            result(dz, p, dc, ab).wait_recv()
    for copy in sends:
        copy.wait_send()
    for k in range(4):
        pass_on(k).wait_send()
        for i in range(3):
            stat_copy(k, i).wait_send()
    for p in range(3):
        for q in range(3):
            for k in range(4):
                stage(p, q, k).wait_send()
    for p in range(3):
        for k in range(4):
            for way in range(2):
                hop(p, k, way).wait_send()
    for dz in range(2):
        for k in range(4):
            y_send(dz, k).wait_send()
            core_send(dz, k).wait_send()
    for i in range(3):
        x_send(i).wait_send()
        left_send(i).wait_send()
        swap(i).wait_send()
    left_core.wait_send()
    for dz, p in parts:
        for dc, ab in mates:
            result(dz, p, dc, ab).wait_send()
    pltpu.make_async_copy(res.at[:, :, 0, 0], got.at[:, :, 0, 0], osem).wait()


def deliver_kernel(got, outputs, block_grad, out, grad_out, tgrad, egrad, mgrad, sgrad, sem):
    r, m, x, y, z, c = place()
    grads = named(tgrad, egrad, mgrad, sgrad)
    out[...] = outputs[...]
    grad_out[...] = block_grad[...]

    def step(w, carry):
        dz, dc, ab = w // 8, (w // 4) % 2, w % 4
        fourth, usual, last = share_columns(*owner_of(y, z, c, ab // 2, ab % 2, dz, dc))

        def start(blocks):
            for j in range(6):
                name, index = blocks[j]
                pltpu.make_async_copy(
                    got.at[dz, j // 2, dc, ab, :, pl.ds(128 * (j % 2), 128)], grads[name].at[:, lanes(index)], sem
                ).start()

        @pl.when(fourth)
        def _():
            start(last)

        @pl.when(jnp.logical_not(fourth))
        def _():
            start(usual)

        return carry

    lax.fori_loop(0, 16, step, 0)
    pltpu.make_async_copy(got, got, sem).wait()


def params(number=None):
    if number is None:
        return pltpu.CompilerParams(vmem_limit_bytes=VMEM_LIMIT)
    return pltpu.CompilerParams(collective_id=number, has_side_effects=True, vmem_limit_bytes=VMEM_LIMIT)


VM = pl.BlockSpec(memory_space=pltpu.VMEM)
HB = pl.BlockSpec(memory_space=pl.ANY)
SEM = pltpu.SemaphoreType.DMA


def shape(*dims, dtype=BF16):
    return jax.ShapeDtypeStruct(dims, dtype)


def block(inp, cot, tri, exp, mer, shr):
    return pl.pallas_call(
        block_kernel,
        out_shape=(shape(64, 384), shape(64, 384), shape(2, 3, 2, 4, 96, 256)),
        in_specs=[VM, VM, HB, HB, HB, HB],
        out_specs=(VM, VM, HB),
        scratch_shapes=[
            pltpu.VMEM((3, 16, 384, 256), BF16),
            pltpu.VMEM((3, 3, 2, 8, 96, 256), BF16),
            pltpu.VMEM((3, 3, 8, 96, 256), BF16),
            pltpu.VMEM((3, 3, 4, 96, 256), BF16),
            pltpu.VMEM((3, 3, 2, 96, 256), BF16),
            pltpu.VMEM((3, 3, 1, 96, 256), BF16),
            pltpu.VMEM((4, 64, 128), F32),
            pltpu.VMEM((4, 3, 64, 128), F32),
            pltpu.VMEM((64, 384), BF16),
            pltpu.VMEM((2, 256, 384), BF16),
            pltpu.VMEM((4, 96, 128), BF16),
            pltpu.VMEM((4, 96, 128), BF16),
            pltpu.VMEM((4, 4, 96, 128), BF16),
            pltpu.VMEM((64, 384), F32),
            pltpu.VMEM((3, 256, 256), F32),
            pltpu.VMEM((3, 256, 256), BF16),
            pltpu.VMEM((2, 4, 2, 3, 256, 256), BF16),
            pltpu.VMEM((2, 256, 384), F32),
            pltpu.VMEM((2, 256, 384), BF16),
            pltpu.VMEM((3, 2, 64, 384), BF16),
            pltpu.VMEM((8, 3, 256, 256), BF16),
            pltpu.VMEM((2, 2, 4, 4, 96, 256), BF16),
            pltpu.VMEM((2, 3, 2, 4, 96, 256), BF16),
            SEM((3,)), SEM((3, 3)), SEM((3, 3)), SEM((4, 3)), SEM((4, 3)), SEM((3, 3, 4)), SEM((3, 3, 4)),
            SEM((3,)), SEM((3,)), SEM((4,)), SEM((4,)),
            SEM((3, 4, 2)), SEM((3, 4, 2)), SEM((2, 4)), SEM((2, 4)), SEM((2, 4)), SEM((2, 4)),
            SEM((4,)), SEM((4,)), SEM((2, 3, 2, 4)), SEM((2, 3, 2, 4)), SEM(()),
        ],
        compiler_params=params(0),
        name="block",
    )(inp, cot, tri, exp, mer, shr)


def deliver(got, outputs, block_grad):
    return pl.pallas_call(
        deliver_kernel,
        out_shape=(
            shape(64, 384), shape(64, 384), shape(3, 96, 1536), shape(96, 3072), shape(96, 1536), shape(96, 3072),
        ),
        in_specs=[VM] * 3,
        out_specs=(VM, VM) + (HB,) * 4,
        scratch_shapes=[SEM(())],
        compiler_params=params(),
        name="deliver",
    )(got, outputs, block_grad)


def body(inputs, triple_weight, expand_weight, merge_weight, shrink_weight, cotangent):
    weights = (triple_weight.transpose(1, 0, 2), expand_weight, merge_weight, shrink_weight)
    outputs, block_grad, got = block(inputs, cotangent, *weights)
    outputs, block_grad, tg, eg, mg, sg = deliver(got, outputs, block_grad)
    return outputs, block_grad, tg.transpose(1, 0, 2), eg, mg, sg


def solution(mesh):
    placed = (
        P(("dp", "my"), "mx"),
        P("mx", None, "my"),
        P("mx", "my"),
        P("mx", "my"),
        P("mx", "my"),
        P(("dp", "my"), "mx"),
    )
    return jax.shard_map(
        body,
        mesh=mesh,
        in_specs=placed,
        out_specs=(
            P(("dp", "my"), "mx"),
            P(("dp", "my"), "mx"),
            P(("mx", "dp"), None, "my"),
            P(("mx", "dp"), "my"),
            P(("mx", "dp"), "my"),
            P(("mx", "dp"), "my"),
        ),
        check_vma=False,
    )
```

```python
import math

import jax
import jax.numpy as jnp
from jax import lax
from jax.experimental import pallas as pl
from jax.experimental.pallas import tpu as pltpu
from jax.sharding import PartitionSpec as P

MESH = pl.DeviceIdType.MESH
F32 = jnp.float32
BF16 = jnp.bfloat16

WIDTH = 6144
EPS = 1e-06
ROOT_HALF = 0.7071067811865476
INV_ROOT_TAU = 0.3989422804014327
SCALE = 1.0 / math.sqrt(128)
VMEM_LIMIT = 60 * 1024 * 1024

SEQ = ((0, 1, 2), (1, 2, 0), (2, 0, 1))
PAIRS = ((0, 2), (1, 3), (4, 5))
CUTS = (((0, 96), (96, 80), (176, 80)), ((0, 80), (80, 96), (176, 80)), ((0, 80), (80, 80), (160, 96)))


def place():
    m = lax.axis_index("mx")
    c = m % 2
    y = (m // 2) % 4
    z = m // 8
    return lax.axis_index("dp"), m, lax.axis_index("my"), y, z, c


def partners(m, y, z, c):
    return (m + 2 * (1 - 2 * (y % 2)), m + 2 * (3 - 2 * y), m + 8 - 16 * z, m + 1 - 2 * c)


def owner_of(y, z, c, da, db, dz, dc):
    b = (y // 2 + db) % 2
    a = (y + y // 2 + da) % 2
    return 2 * b + (a + b) % 2, (z + dz) % 2, (c + dc) % 2


def share_columns(yo, zo, co):
    k = zo * 2 + co
    head = 3 * yo + k
    unit = 6 * yo + k
    usual = (("s", unit), ("m", head), ("e", unit), ("q", head), ("k", head), ("v", head))
    first = 6 * yo + 3
    fourth = (("s", first), ("s", first + 1), ("e", first), ("s", first + 2), ("e", first + 1), ("e", first + 2))
    return k == 3, usual, fourth


def named(tri, exp, mer, shr):
    return {"q": tri.at[0], "k": tri.at[1], "v": tri.at[2], "e": exp, "m": mer, "s": shr}


def lanes(index):
    return pl.ds(pl.multiple_of(index * 128, 128), 128)


def load_weights(p, refs, held, sem, y, z, c):
    def step(s, carry):
        yo, zo, co = owner_of(y, z, c, s // 8, (s // 4) % 2, (s // 2) % 2, s % 2)
        fourth, usual, last = share_columns(yo, zo, co)

        def start(blocks):
            for half in range(2):
                name, index = blocks[2 * p + half]
                pltpu.make_async_copy(
                    refs[name].at[:, lanes(index)], held.at[p, s, :, pl.ds(128 * half, 128)], sem.at[p]
                ).start()

        @pl.when(fourth)
        def _():
            start(last)

        @pl.when(jnp.logical_not(fourth))
        def _():
            start(usual)

        return carry

    lax.fori_loop(0, 16, step, 0)


def wait_weights(p, held, sem):
    pltpu.make_async_copy(held.at[p], held.at[p], sem.at[p]).wait()


def remote(src, dst, send, recv, device):
    return pltpu.make_async_remote_copy(
        src_ref=src, dst_ref=dst, send_sem=send, recv_sem=recv, device_id=device, device_id_type=MESH
    )


def greet(devices):
    barrier = pltpu.get_barrier_semaphore()
    for device in devices:
        pl.semaphore_signal(barrier, inc=1, device_id=device, device_id_type=MESH)
    pl.semaphore_wait(barrier, len(devices))


def dot_last(left, right):
    return lax.dot_general(left, right, (((1,), (1,)), ((), ())), preferred_element_type=F32)


def dot_first(left, right):
    return lax.dot_general(left, right, (((0,), (0,)), ((), ())), preferred_element_type=F32)


def norm_heads(block):
    centre = block - jnp.mean(block, axis=-1, keepdims=True)
    inverse = lax.rsqrt(jnp.mean(centre * centre, axis=-1, keepdims=True) + EPS)
    return centre * inverse, inverse


def norm_backward(grad, unit, inverse):
    first = jnp.mean(grad, axis=-1, keepdims=True)
    second = jnp.mean(grad * unit, axis=-1, keepdims=True)
    return (grad - first - unit * second) * inverse


def gelu_pair(pre):
    phi = 0.5 * (1.0 + lax.erf(pre * ROOT_HALF))
    return pre * phi, phi + pre * jnp.exp(-0.5 * pre * pre) * INV_ROOT_TAU


LEFT = slice(0, 128)
RIGHT = slice(128, 256)


def hidden_unit(proj, out, pre_at, grad_at, value_to, slope_to):
    value, slope = gelu_pair(proj[pre_at[0], :, pre_at[1]])
    grad = proj[grad_at[0], :, grad_at[1]]
    out[value_to[0], :, value_to[1]] = value.astype(BF16)
    out[slope_to[0], :, slope_to[1]] = (grad * slope).astype(BF16)


def middle(proj, out, fourth):
    @pl.when(fourth)
    def _():
        hidden_unit(proj, out, (2, LEFT), (0, RIGHT), (1, LEFT), (2, LEFT))
        hidden_unit(proj, out, (2, RIGHT), (1, RIGHT), (1, RIGHT), (2, RIGHT))

    @pl.when(jnp.logical_not(fourth))
    def _():
        qhat, qinv = norm_heads(proj[1, :, RIGHT])
        khat, kinv = norm_heads(proj[2, :, LEFT])
        q, k = qhat.astype(BF16), khat.astype(BF16)
        v = proj[2, :, RIGHT].astype(BF16)
        datt = proj[0, :, RIGHT].astype(BF16)
        expo = jnp.exp(dot_last(q, k) * SCALE)
        probs = expo / jnp.sum(expo, axis=-1, keepdims=True)
        half = probs.astype(BF16)
        out[1, :, LEFT] = jnp.dot(half, v, preferred_element_type=F32).astype(BF16)
        g = dot_last(datt, v)
        ds = (probs * (g - jnp.sum(probs * g, axis=-1, keepdims=True))).astype(BF16)
        dqn = jnp.dot(ds, k, preferred_element_type=F32) * SCALE
        dkn = dot_first(ds, q) * SCALE
        out[1, :, RIGHT] = norm_backward(dqn, qhat, qinv).astype(BF16)
        out[2, :, LEFT] = norm_backward(dkn, khat, kinv).astype(BF16)
        out[2, :, RIGHT] = dot_first(half, datt).astype(BF16)


def block_kernel(
    inp, cot, tri, exp, mer, shr, outputs, block_grad, got,
    held, part, got0, got1, got2, got3, stat_out, stat_in, nown, both, turned, mixed, spread, hat, proj, down,
    slots, acc, xsend, xgot, ring, left, res,
    wsem, xs, xr, ss, sr, rs, rr, es, er, fs, fr, zs, zr, ys, yr, cs, cr, ls, lr, gs, gr, osem,
):
    r, m, x, y, z, c = place()
    refs = named(tri, exp, mer, shr)
    peers = partners(m, y, z, c)
    xpeers = [(x + i) % 4 for i in (1, 2, 3)]
    rpeers = [(r + i) % 4 for i in (1, 2, 3)]
    inner = m % 8
    up = {"dp": (r + z) % 4, "mx": inner + 8 * (1 - z)}
    below = {"dp": (r + 3 + z) % 4, "mx": inner + 8 * (1 - z)}
    other_core = 1 - 2 * c
    opposite = (m + 4) % 8 + 8 * z
    near = (None, peers[1], peers[0], opposite)

    def mate(dc, ab):
        base = m if ab == 0 else near[ab]
        return {"mx": base + other_core if dc else base}

    mates = [(dc, ab) for ab in (3, 2, 1, 0) for dc in (0, 1) if dc or ab]
    rounds = (
        ({"mx": peers[3]}, {"mx": peers[2]}, {"mx": peers[2] + other_core}),
        ({"mx": peers[0]}, {"mx": peers[1]}, {"mx": opposite}),
    )
    greet(
        [{"my": q} for q in xpeers] + [{"dp": q} for q in rpeers] + [up, below, rounds[0][2]]
        + [mate(dc, ab) for dc, ab in mates]
    )

    own = pl.ds(pl.multiple_of(x * 64, 64), 64)
    sends = []
    for i in range(3):
        copy = remote(cot, both.at[1, own], xs.at[0, i], xr.at[0, i], {"my": xpeers[i]})
        copy.start()
        sends.append(copy)
    both[1, own, :] = cot[...]

    rows = inp[...].astype(F32)
    mean = jnp.sum(rows, axis=1, keepdims=True) / rows.shape[1]
    centred = rows - mean
    square = jnp.sum(centred * centred, axis=1, keepdims=True)
    low = lax.broadcasted_iota(jnp.int32, (64, 128), 1) < 64

    def stat_copy(k, i):
        return remote(stat_out.at[k], stat_in.at[k, i], ss.at[k, i], sr.at[k, i], rounds[k % 2][i])

    def stat_start(k, pair):
        stat_out[k] = jnp.where(low, pair[0], pair[1])
        for i in range(3):
            stat_copy(k, i).start()

    def stat_finish(k):
        pairs = []
        for i in range(3):
            stat_copy(k, i).wait_recv()
            pairs.append((stat_in[k, i, :, 0:1], stat_in[k, i, :, 64:65]))
        return pairs

    def combine(own_pair, pairs, count):
        pairs = [own_pair] + pairs
        middle_of = sum(pair[0] for pair in pairs) / 4
        spread_of = sum(pair[1] + count * (pair[0] - middle_of) ** 2 for pair in pairs)
        return middle_of, spread_of

    pair = (mean, square)
    stat_start(0, pair)
    load_weights(0, refs, held, wsem, y, z, c)
    pair = combine(pair, stat_finish(0), 384.0)
    stat_start(1, pair)

    def gathered(k):
        for i in range(3):
            rows_of = both.at[1 - k, pl.ds(pl.multiple_of(((x + 3 - i) % 4) * 64, 64), 64)]
            remote(rows_of, rows_of, xs.at[k, i], xr.at[k, i], {"my": xpeers[i]}).wait_recv()

    def multiply(p, dc):
        def step(t, carry):
            da, db, dz = t // 4, (t // 2) % 2, t % 2
            s = t * 2 + dc
            places = (t, 4 * db + 2 * dz + da, 4 * dz + 2 * da + db)

            def put(value, columns):
                for q in range(3):
                    at, size = CUTS[p][q]
                    part[p, q, dc, places[q], 0:size, columns] = value[at : at + size]

            if p == 1:
                fourth = ((z + dz) % 2) * ((c + dc) % 2)
                first = jnp.dot(both[0], held[p, s, :, 0:128], preferred_element_type=F32)
                second = jnp.dot(both[fourth], held[p, s, :, 128:256], preferred_element_type=F32)
                put(first.astype(BF16), slice(0, 128))
                put(second.astype(BF16), slice(128, 256))
            else:
                full = both[1 if p == 0 else 0]
                put(jnp.dot(full, held[p, s], preferred_element_type=F32).astype(BF16), slice(0, 256))
            return carry

        lax.fori_loop(0, 8, step, 0)

    def stage(p, q, k):
        size = CUTS[p][q][1]
        sem = (rs.at[p, q, k], rr.at[p, q, k])
        if k == 0:
            return remote(part.at[p, q, 1, :, 0:size], got0.at[p, q, :, 0:size], *sem, {"mx": peers[3]})
        slots = 8 >> k
        target = (None, got1, got2, got3)[k]
        return remote(
            part.at[p, q, 0, pl.ds(slots, slots), 0:size], target.at[p, q, :, 0:size], *sem,
            {"mx": peers[SEQ[q][k - 1]]},
        )

    def begin(p):
        for q in range(3):
            stage(p, q, 0).start()

    def advance(p, k):
        source = (got0, got1, got2, got3)[k]
        for q in range(3):
            at, size = CUTS[p][q]
            stage(p, q, k).wait_recv()

            def step(t, carry):
                total = part[p, q, 0, t, 0:size].astype(F32) + source[p, q, t, 0:size].astype(F32)
                part[p, q, 0, t, 0:size] = total.astype(BF16)
                return carry

            if k < 3:
                lax.fori_loop(0, 8 >> k, step, 0)
                stage(p, q, k + 1).start()
            else:
                proj[p, at : at + size] = (
                    part[p, q, 0, 0, 0:size].astype(F32) + source[p, q, 0, 0:size].astype(F32)
                )

    def swap(i):
        q = rpeers[i]
        return remote(turned.at[q], mixed.at[3 - i], es.at[i], er.at[i], {"dp": q})

    def pass_on(k):
        sem = (fs.at[k], fr.at[k])
        if k == 0:
            return remote(mixed, spread.at[:, 2], *sem, {"mx": peers[0]})
        if k == 1:
            return remote(mixed, spread.at[:, 1], *sem, {"mx": peers[1]})
        if k == 2:
            return remote(spread.at[0:2, 2], spread.at[0:2, 3], *sem, {"mx": peers[1]})
        return remote(spread.at[2:4, 1], spread.at[2:4, 3], *sem, {"mx": peers[0]})

    top, bottom = pl.ds(0, 128), pl.ds(128, 128)

    def hop(p, k, way):
        sem = (zs.at[p, k, way], zr.at[p, k, way])
        if way == 0:
            src = down.at[p] if k == 0 else ring.at[8 - k, p]
            dst = ring.at[7 - k, p]
            if k == 3:
                src, dst = src.at[top], dst.at[top]
            return remote(src, dst, *sem, up)
        src = down.at[p] if k == 0 else ring.at[k, p]
        dst = ring.at[k + 1, p]
        if k == 3:
            src, dst = src.at[bottom], dst.at[bottom]
        return remote(src, dst, *sem, below)

    def hop_start(p, k):
        hop(p, k, 0).start()
        hop(p, k, 1).start()

    def hop_wait(p, k):
        hop(p, k, 0).wait_recv()
        hop(p, k, 1).wait_recv()

    def share(p, dz):
        return down.at[p] if dz == 0 else ring.at[1 + 6 * z, p]

    def y_send(p, dz, k):
        sem = (ys.at[p, dz, k], yr.at[p, dz, k])
        if k == 0:
            return remote(share(p, dz), slots.at[dz, 2, 0, p], *sem, {"mx": peers[0]})
        if k == 1:
            return remote(share(p, dz), slots.at[dz, 1, 0, p], *sem, {"mx": peers[1]})
        if k == 2:
            return remote(slots.at[dz, 2, 0, p, top], slots.at[dz, 3, 0, p, top], *sem, {"mx": peers[1]})
        return remote(slots.at[dz, 1, 0, p, bottom], slots.at[dz, 3, 0, p, bottom], *sem, {"mx": peers[0]})

    def core_send(p, dz, ab):
        src = slots.at[dz, ab, 0, p] if ab else share(p, dz)
        return remote(src, slots.at[dz, ab, 1, p], cs.at[p, dz, ab], cr.at[p, dz, ab], {"mx": peers[3]})

    def spread_share(p, dz):
        y_send(p, dz, 0).start()
        y_send(p, dz, 1).start()
        core_send(p, dz, 0).start()

    def pass_share(p, dz):
        y_send(p, dz, 0).wait_recv()
        y_send(p, dz, 2).start()
        core_send(p, dz, 2).start()
        y_send(p, dz, 1).wait_recv()
        y_send(p, dz, 3).start()
        core_send(p, dz, 1).start()

    def last_share(p, dz):
        y_send(p, dz, 2).wait_recv()
        y_send(p, dz, 3).wait_recv()
        core_send(p, dz, 3).start()

    def left_at(q):
        return left.at[q // 2, 0, :, :, :, lanes(q % 2)]

    def left_send(i):
        return remote(spread, left_at(x), ls.at[i], lr.at[i], {"my": xpeers[i]})

    left_core = remote(left.at[:, 0], left.at[:, 1], ls.at[3], lr.at[3], {"mx": peers[3]})

    def dgrad(data, dz, ab, dc):
        s = ab * 4 + dz * 2 + dc
        fourth = ((z + dz) % 2) * ((c + dc) % 2)
        values = jnp.concatenate([data[0, :, LEFT], data[1, :, LEFT]], axis=1)
        acc[0] += dot_last(values, held[0, s])
        acc[1] += dot_last(data[0, :, RIGHT], held[1, s, :, LEFT]) + dot_last(data[2], held[2, s])
        acc[1 - fourth] += dot_last(data[1, :, RIGHT], held[1, s, :, RIGHT])

    def use(dz, ab):
        dgrad(slots.at[dz, ab, 0], dz, ab, 0)

    def use_other(dz, ab):
        for p in range(3):
            core_send(p, dz, ab).wait_recv()
        dgrad(slots.at[dz, ab, 1], dz, ab, 1)

    def result(dz, p, dc, ab):
        return remote(
            res.at[dz, p, dc, ab], got.at[dz, p, dc, ab], gs.at[dz, p, dc, ab], gr.at[dz, p, dc, ab], mate(dc, ab)
        )

    def weight_part(dz, p):
        fourth = ((z + dz) % 2) * c

        def total(dc, side, columns):
            sum_of = None
            for k in range(4):
                d = (dz * (1 + 6 * z) + 2 * k) % 8
                term = jnp.dot(
                    left[side, dc, k].reshape(384, 256), ring[d, p, :, columns], preferred_element_type=F32
                )
                sum_of = term if sum_of is None else sum_of + term
            return sum_of.astype(BF16).reshape(4, 96, -1)

        for dc in range(2):
            if p < 2:
                res[dz, p, dc, :, :, LEFT] = total(dc, 1, LEFT)
                res[dz, p, dc, :, :, RIGHT] = total(dc, fourth if p else 0, RIGHT)
            else:
                res[dz, p, dc] = total(dc, 0, slice(0, 256))
        pltpu.make_async_copy(res.at[dz, p, 0, 0], got.at[dz, p, 0, 0], osem).start()
        for dc, ab in mates:
            result(dz, p, dc, ab).start()

    def x_send(i):
        rows_of = pl.ds(pl.multiple_of(xpeers[i] * 64, 64), 64)
        return remote(xsend.at[:, rows_of], xgot.at[i], xs.at[2, i], xr.at[2, i], {"my": xpeers[i]})

    gathered(0)
    wait_weights(0, held, wsem)
    multiply(0, 1)
    begin(0)
    pair = combine(pair, stat_finish(1), 1536.0)
    inverse = lax.rsqrt(pair[1] / WIDTH + EPS)
    unit = (rows - pair[0]) * inverse
    nown[...] = unit.astype(BF16)
    both[0, own, :] = unit.astype(BF16)
    for i in range(3):
        copy = remote(nown, both.at[0, own], xs.at[1, i], xr.at[1, i], {"my": xpeers[i]})
        copy.start()
        sends.append(copy)
    hat[...] = unit
    multiply(0, 0)
    load_weights(1, refs, held, wsem, y, z, c)
    advance(0, 0)
    load_weights(2, refs, held, wsem, y, z, c)
    advance(0, 1)
    gathered(1)
    wait_weights(1, held, wsem)
    multiply(1, 1)
    begin(1)
    multiply(1, 0)
    wait_weights(2, held, wsem)
    advance(1, 0)
    multiply(2, 1)
    begin(2)
    advance(0, 2)

    quarter = both[x // 2, pl.ds(pl.multiple_of((x % 2) * 128, 128), 128), :]
    turned[...] = quarter.T.reshape(4, 96, 128)
    for i in range(3):
        swap(i).start()
    mixed[0] = turned[r]
    multiply(2, 0)
    advance(1, 1)
    advance(2, 0)
    advance(1, 2)
    advance(0, 3)
    for i in range(3):
        swap(i).wait_recv()
    pass_on(0).start()
    pass_on(1).start()
    spread[:, 0] = mixed[...]
    advance(2, 1)
    advance(1, 3)

    hidden_unit(proj, down, (1, LEFT), (0, LEFT), (0, LEFT), (0, RIGHT))
    hop_start(0, 0)
    spread_share(0, 0)
    ring[0, 0] = down[0]
    pass_on(0).wait_recv()
    pass_on(2).start()
    pass_on(1).wait_recv()
    pass_on(3).start()
    advance(2, 2)
    acc[...] = jnp.zeros_like(acc)
    hop_wait(0, 0)
    hop_start(0, 1)
    spread_share(0, 1)
    pass_on(2).wait_recv()
    pass_on(3).wait_recv()
    for i in range(3):
        left_send(i).start()
    left[x // 2, 0, :, :, :, lanes(x % 2)] = spread[...]
    advance(2, 3)
    pass_share(0, 0)
    middle(proj, down, z * 2 + c == 3)

    for p in (1, 2):
        hop_start(p, 0)
    for p in (1, 2):
        spread_share(p, 0)
    ring[0, 1:3] = down[1:3]
    hop_wait(0, 1)
    hop_start(0, 2)
    dgrad(down, 0, 0, 0)
    pass_share(0, 1)
    last_share(0, 0)
    for p in (1, 2):
        hop_wait(p, 0)
        hop_start(p, 1)
        spread_share(p, 1)
    hop_wait(0, 2)
    hop_start(0, 3)
    use_other(0, 0)
    dgrad(ring.at[1 + 6 * z], 1, 0, 0)
    for p in (1, 2):
        pass_share(p, 0)
    use(0, 2)
    use(0, 1)
    for i in range(3):
        remote(spread, left_at((x + 3 - i) % 4), ls.at[i], lr.at[i], {"my": xpeers[i]}).wait_recv()
    left_core.start()
    for p in (1, 2):
        hop_wait(p, 1)
        hop_start(p, 2)
    last_share(0, 1)
    hop_wait(0, 3)
    use_other(1, 0)
    left_core.wait_recv()
    weight_part(0, 0)
    weight_part(1, 0)
    for p in (1, 2):
        pass_share(p, 1)
        last_share(p, 0)
    for p in (1, 2):
        hop_wait(p, 2)
        hop_start(p, 3)
    use(0, 3)
    use_other(0, 2)
    use_other(0, 1)
    hop_wait(1, 3)
    weight_part(0, 1)
    weight_part(1, 1)
    hop_wait(2, 3)
    weight_part(0, 2)
    weight_part(1, 2)
    for p in (1, 2):
        last_share(p, 1)
    use(1, 2)
    use(1, 1)
    use(1, 3)
    use_other(0, 3)
    for ab in (2, 1, 3):
        use_other(1, ab)

    xsend[...] = acc[...].astype(BF16)
    for i in range(3):
        x_send(i).start()
    own = pl.ds(pl.multiple_of(x * 64, 64), 64)
    branch = acc[0, own, :]
    grad = acc[1, own, :]
    for i in range(3):
        x_send(i).wait_recv()
        branch = branch + xgot[i, 0].astype(F32)
        grad = grad + xgot[i, 1].astype(F32)
    outputs[...] = (inp[...].astype(F32) + branch).astype(BF16)
    unit = hat[...]
    sums = (jnp.sum(grad, axis=1, keepdims=True), jnp.sum(grad * unit, axis=1, keepdims=True))
    for k in (2, 3):
        stat_start(k, sums)
        for pair in stat_finish(k):
            sums = (sums[0] + pair[0], sums[1] + pair[1])
    fixed = (grad - sums[0] / WIDTH - unit * (sums[1] / WIDTH)) * inverse
    block_grad[...] = (cot[...].astype(F32) + fixed).astype(BF16)

    parts = [(dz, p) for p in range(3) for dz in range(2)]
    for dz, p in parts:
        for dc, ab in mates:
            result(dz, p, dc, ab).wait_recv()
    for copy in sends:
        copy.wait_send()
    for k in range(4):
        pass_on(k).wait_send()
        for i in range(3):
            stat_copy(k, i).wait_send()
    for p in range(3):
        for q in range(3):
            for k in range(4):
                stage(p, q, k).wait_send()
    for p in range(3):
        for k in range(4):
            for way in range(2):
                hop(p, k, way).wait_send()
            for dz in range(2):
                y_send(p, dz, k).wait_send()
                core_send(p, dz, k).wait_send()
    for i in range(3):
        x_send(i).wait_send()
        left_send(i).wait_send()
        swap(i).wait_send()
    left_core.wait_send()
    for dz, p in parts:
        for dc, ab in mates:
            result(dz, p, dc, ab).wait_send()
    pltpu.make_async_copy(res.at[:, :, 0, 0], got.at[:, :, 0, 0], osem).wait()


def deliver_kernel(got, outputs, block_grad, out, grad_out, tgrad, egrad, mgrad, sgrad, sem):
    r, m, x, y, z, c = place()
    grads = named(tgrad, egrad, mgrad, sgrad)
    out[...] = outputs[...]
    grad_out[...] = block_grad[...]

    def step(w, carry):
        dz, dc, ab = w // 8, (w // 4) % 2, w % 4
        fourth, usual, last = share_columns(*owner_of(y, z, c, ab // 2, ab % 2, dz, dc))

        def start(blocks):
            for j in range(6):
                name, index = blocks[PAIRS[j // 2][j % 2]]
                pltpu.make_async_copy(
                    got.at[dz, j // 2, dc, ab, :, pl.ds(128 * (j % 2), 128)], grads[name].at[:, lanes(index)], sem
                ).start()

        @pl.when(fourth)
        def _():
            start(last)

        @pl.when(jnp.logical_not(fourth))
        def _():
            start(usual)

        return carry

    lax.fori_loop(0, 16, step, 0)
    pltpu.make_async_copy(got, got, sem).wait()


def params(number=None):
    if number is None:
        return pltpu.CompilerParams(vmem_limit_bytes=VMEM_LIMIT)
    return pltpu.CompilerParams(collective_id=number, has_side_effects=True, vmem_limit_bytes=VMEM_LIMIT)


VM = pl.BlockSpec(memory_space=pltpu.VMEM)
HB = pl.BlockSpec(memory_space=pl.ANY)
SEM = pltpu.SemaphoreType.DMA


def shape(*dims, dtype=BF16):
    return jax.ShapeDtypeStruct(dims, dtype)


def block(inp, cot, tri, exp, mer, shr):
    return pl.pallas_call(
        block_kernel,
        out_shape=(shape(64, 384), shape(64, 384), shape(2, 3, 2, 4, 96, 256)),
        in_specs=[VM, VM, HB, HB, HB, HB],
        out_specs=(VM, VM, HB),
        scratch_shapes=[
            pltpu.VMEM((3, 16, 384, 256), BF16),
            pltpu.VMEM((3, 3, 2, 8, 96, 256), BF16),
            pltpu.VMEM((3, 3, 8, 96, 256), BF16),
            pltpu.VMEM((3, 3, 4, 96, 256), BF16),
            pltpu.VMEM((3, 3, 2, 96, 256), BF16),
            pltpu.VMEM((3, 3, 1, 96, 256), BF16),
            pltpu.VMEM((4, 64, 128), F32),
            pltpu.VMEM((4, 3, 64, 128), F32),
            pltpu.VMEM((64, 384), BF16),
            pltpu.VMEM((2, 256, 384), BF16),
            pltpu.VMEM((4, 96, 128), BF16),
            pltpu.VMEM((4, 96, 128), BF16),
            pltpu.VMEM((4, 4, 96, 128), BF16),
            pltpu.VMEM((64, 384), F32),
            pltpu.VMEM((3, 256, 256), F32),
            pltpu.VMEM((3, 256, 256), BF16),
            pltpu.VMEM((2, 4, 2, 3, 256, 256), BF16),
            pltpu.VMEM((2, 256, 384), F32),
            pltpu.VMEM((2, 256, 384), BF16),
            pltpu.VMEM((3, 2, 64, 384), BF16),
            pltpu.VMEM((8, 3, 256, 256), BF16),
            pltpu.VMEM((2, 2, 4, 4, 96, 256), BF16),
            pltpu.VMEM((2, 3, 2, 4, 96, 256), BF16),
            SEM((3,)), SEM((3, 3)), SEM((3, 3)), SEM((4, 3)), SEM((4, 3)), SEM((3, 3, 4)), SEM((3, 3, 4)),
            SEM((3,)), SEM((3,)), SEM((4,)), SEM((4,)),
            SEM((3, 4, 2)), SEM((3, 4, 2)), SEM((3, 2, 4)), SEM((3, 2, 4)), SEM((3, 2, 4)), SEM((3, 2, 4)),
            SEM((4,)), SEM((4,)), SEM((2, 3, 2, 4)), SEM((2, 3, 2, 4)), SEM(()),
        ],
        compiler_params=params(0),
        name="block",
    )(inp, cot, tri, exp, mer, shr)


def deliver(got, outputs, block_grad):
    return pl.pallas_call(
        deliver_kernel,
        out_shape=(
            shape(64, 384), shape(64, 384), shape(3, 96, 1536), shape(96, 3072), shape(96, 1536), shape(96, 3072),
        ),
        in_specs=[VM] * 3,
        out_specs=(VM, VM) + (HB,) * 4,
        scratch_shapes=[SEM(())],
        compiler_params=params(),
        name="deliver",
    )(got, outputs, block_grad)


def body(inputs, triple_weight, expand_weight, merge_weight, shrink_weight, cotangent):
    weights = (triple_weight.transpose(1, 0, 2), expand_weight, merge_weight, shrink_weight)
    outputs, block_grad, got = block(inputs, cotangent, *weights)
    outputs, block_grad, tg, eg, mg, sg = deliver(got, outputs, block_grad)
    return outputs, block_grad, tg.transpose(1, 0, 2), eg, mg, sg


def solution(mesh):
    placed = (
        P(("dp", "my"), "mx"),
        P("mx", None, "my"),
        P("mx", "my"),
        P("mx", "my"),
        P("mx", "my"),
        P(("dp", "my"), "mx"),
    )
    return jax.shard_map(
        body,
        mesh=mesh,
        in_specs=placed,
        out_specs=(
            P(("dp", "my"), "mx"),
            P(("dp", "my"), "mx"),
            P(("mx", "dp"), None, "my"),
            P(("mx", "dp"), "my"),
            P(("mx", "dp"), "my"),
            P(("mx", "dp"), "my"),
        ),
        check_vma=False,
    )
```

```python
import math

import jax
import jax.numpy as jnp
from jax import lax
from jax.experimental import pallas as pl
from jax.experimental.pallas import tpu as pltpu
from jax.sharding import PartitionSpec as P

MESH = pl.DeviceIdType.MESH
F32 = jnp.float32
BF16 = jnp.bfloat16

WIDTH = 6144
EPS = 1e-06
ROOT_HALF = 0.7071067811865476
INV_ROOT_TAU = 0.3989422804014327
SCALE = 1.0 / math.sqrt(128)
VMEM_LIMIT = 60 * 1024 * 1024

SEQ = ((0, 1, 2), (1, 2, 0), (2, 0, 1))
PAIRS = ((0, 2), (1, 3), (4, 5))
CUTS = (((0, 96), (96, 80), (176, 80)), ((0, 80), (80, 96), (176, 80)), ((0, 80), (80, 80), (160, 96)))


def place():
    m = lax.axis_index("mx")
    c = m % 2
    y = (m // 2) % 4
    z = m // 8
    return lax.axis_index("dp"), m, lax.axis_index("my"), y, z, c


def partners(m, y, z, c):
    return (m + 2 * (1 - 2 * (y % 2)), m + 2 * (3 - 2 * y), m + 8 - 16 * z, m + 1 - 2 * c)


def owner_of(y, z, c, da, db, dz, dc):
    b = (y // 2 + db) % 2
    a = (y + y // 2 + da) % 2
    return 2 * b + (a + b) % 2, (z + dz) % 2, (c + dc) % 2


def share_columns(yo, zo, co):
    k = zo * 2 + co
    head = 3 * yo + k
    unit = 6 * yo + k
    usual = (("s", unit), ("m", head), ("e", unit), ("q", head), ("k", head), ("v", head))
    first = 6 * yo + 3
    fourth = (("s", first), ("s", first + 1), ("e", first), ("s", first + 2), ("e", first + 1), ("e", first + 2))
    return k == 3, usual, fourth


def named(tri, exp, mer, shr):
    return {"q": tri.at[0], "k": tri.at[1], "v": tri.at[2], "e": exp, "m": mer, "s": shr}


def lanes(index):
    return pl.ds(pl.multiple_of(index * 128, 128), 128)


def load_weights(p, refs, held, sem, y, z, c):
    def step(s, carry):
        yo, zo, co = owner_of(y, z, c, s // 8, (s // 4) % 2, (s // 2) % 2, s % 2)
        fourth, usual, last = share_columns(yo, zo, co)

        def start(blocks):
            for half in range(2):
                name, index = blocks[2 * p + half]
                pltpu.make_async_copy(
                    refs[name].at[:, lanes(index)], held.at[p, s, :, pl.ds(128 * half, 128)], sem.at[p]
                ).start()

        @pl.when(fourth)
        def _():
            start(last)

        @pl.when(jnp.logical_not(fourth))
        def _():
            start(usual)

        return carry

    lax.fori_loop(0, 16, step, 0)


def wait_weights(p, held, sem):
    pltpu.make_async_copy(held.at[p], held.at[p], sem.at[p]).wait()


def remote(src, dst, send, recv, device):
    return pltpu.make_async_remote_copy(
        src_ref=src, dst_ref=dst, send_sem=send, recv_sem=recv, device_id=device, device_id_type=MESH
    )


def greet(devices):
    barrier = pltpu.get_barrier_semaphore()
    for device in devices:
        pl.semaphore_signal(barrier, inc=1, device_id=device, device_id_type=MESH)
    pl.semaphore_wait(barrier, len(devices))


def dot_last(left, right):
    return lax.dot_general(left, right, (((1,), (1,)), ((), ())), preferred_element_type=F32)


def dot_first(left, right):
    return lax.dot_general(left, right, (((0,), (0,)), ((), ())), preferred_element_type=F32)


def norm_heads(block):
    centre = block - jnp.mean(block, axis=-1, keepdims=True)
    inverse = lax.rsqrt(jnp.mean(centre * centre, axis=-1, keepdims=True) + EPS)
    return centre * inverse, inverse


def norm_backward(grad, unit, inverse):
    first = jnp.mean(grad, axis=-1, keepdims=True)
    second = jnp.mean(grad * unit, axis=-1, keepdims=True)
    return (grad - first - unit * second) * inverse


def gelu_pair(pre):
    phi = 0.5 * (1.0 + lax.erf(pre * ROOT_HALF))
    return pre * phi, phi + pre * jnp.exp(-0.5 * pre * pre) * INV_ROOT_TAU


LEFT = slice(0, 128)
RIGHT = slice(128, 256)


def hidden_unit(proj, out, pre_at, grad_at, value_to, slope_to):
    value, slope = gelu_pair(proj[pre_at[0], :, pre_at[1]])
    grad = proj[grad_at[0], :, grad_at[1]]
    out[value_to[0], :, value_to[1]] = value.astype(BF16)
    out[slope_to[0], :, slope_to[1]] = (grad * slope).astype(BF16)


def middle(proj, out, fourth):
    @pl.when(fourth)
    def _():
        hidden_unit(proj, out, (2, LEFT), (0, RIGHT), (1, LEFT), (2, LEFT))
        hidden_unit(proj, out, (2, RIGHT), (1, RIGHT), (1, RIGHT), (2, RIGHT))

    @pl.when(jnp.logical_not(fourth))
    def _():
        qhat, qinv = norm_heads(proj[1, :, RIGHT])
        khat, kinv = norm_heads(proj[2, :, LEFT])
        q, k = qhat.astype(BF16), khat.astype(BF16)
        v = proj[2, :, RIGHT].astype(BF16)
        datt = proj[0, :, RIGHT].astype(BF16)
        expo = jnp.exp(dot_last(q, k) * SCALE)
        probs = expo / jnp.sum(expo, axis=-1, keepdims=True)
        half = probs.astype(BF16)
        out[1, :, LEFT] = jnp.dot(half, v, preferred_element_type=F32).astype(BF16)
        g = dot_last(datt, v)
        ds = (probs * (g - jnp.sum(probs * g, axis=-1, keepdims=True))).astype(BF16)
        dqn = jnp.dot(ds, k, preferred_element_type=F32) * SCALE
        dkn = dot_first(ds, q) * SCALE
        out[1, :, RIGHT] = norm_backward(dqn, qhat, qinv).astype(BF16)
        out[2, :, LEFT] = norm_backward(dkn, khat, kinv).astype(BF16)
        out[2, :, RIGHT] = dot_first(half, datt).astype(BF16)


def block_kernel(
    inp, cot, tri, exp, mer, shr, outputs, block_grad, got,
    held, part, got0, got1, got2, got3, stat_out, stat_in, row_stats, local, stat_near, stat_all, col_sums, sums_near,
    sums_all, stat_cols, nown, both, turned, mixed, spread, hat, proj, down,
    slots, acc, xsend, xgot, ring, left, res,
    wsem, xs, xr, ss, sr, ns, nr, rs, rr, es, er, fs, fr, zs, zr, ys, yr, cs, cr, ls, lr, gs, gr, osem,
):
    r, m, x, y, z, c = place()
    refs = named(tri, exp, mer, shr)
    peers = partners(m, y, z, c)
    xpeers = [(x + i) % 4 for i in (1, 2, 3)]
    rpeers = [(r + i) % 4 for i in (1, 2, 3)]
    inner = m % 8
    up = {"dp": (r + z) % 4, "mx": inner + 8 * (1 - z)}
    below = {"dp": (r + 3 + z) % 4, "mx": inner + 8 * (1 - z)}
    other_core = 1 - 2 * c
    opposite = (m + 4) % 8 + 8 * z
    near = (None, peers[1], peers[0], opposite)

    def mate(dc, ab):
        base = m if ab == 0 else near[ab]
        return {"mx": base + other_core if dc else base}

    mates = [(dc, ab) for ab in (3, 2, 1, 0) for dc in (0, 1) if dc or ab]
    rounds = (
        ({"mx": peers[3]}, {"mx": peers[2]}, {"mx": peers[2] + other_core}),
        ({"mx": peers[0]}, {"mx": peers[1]}, {"mx": opposite}),
    )
    load_weights(0, refs, held, wsem, y, z, c)

    rows = inp[...].astype(F32)
    mean = jnp.sum(rows, axis=1, keepdims=True) / rows.shape[1]
    centred = rows - mean
    square = jnp.sum(centred * centred, axis=1, keepdims=True)
    low = lax.broadcasted_iota(jnp.int32, (64, 128), 1) < 64
    nown[0] = centred.astype(BF16)
    local[...] = jnp.where(low, mean, square)
    greet(
        [{"my": q} for q in xpeers] + [{"dp": q} for q in rpeers] + [up, below, rounds[0][2]]
        + [mate(dc, ab) for dc, ab in mates]
    )

    own = pl.ds(pl.multiple_of(x * 64, 64), 64)
    sends = []

    def to_rows(k, src, full):
        for i in range(3):
            copy = remote(src, full.at[own], xs.at[k, i], xr.at[k, i], {"my": xpeers[i]})
            copy.start()
            sends.append(copy)
        full[own, :] = src[...]

    def gathered(k, full):
        for i in range(3):
            rows_of = full.at[pl.ds(pl.multiple_of(((x + 3 - i) % 4) * 64, 64), 64)]
            remote(rows_of, rows_of, xs.at[k, i], xr.at[k, i], {"my": xpeers[i]}).wait_recv()

    to_rows(0, cot, both.at[1])
    to_rows(1, nown.at[0], both.at[0])
    to_rows(3, local, row_stats)
    both[0, 256:272, :] = jnp.ones((16, 384), BF16)
    col_sums[...] = jnp.zeros_like(col_sums)

    def stat_copy(k, i):
        return remote(stat_out.at[k], stat_in.at[k, i], ss.at[k, i], sr.at[k, i], rounds[k % 2][i])

    def stat_start(k, pair):
        stat_out[k] = jnp.where(low, pair[0], pair[1])
        for i in range(3):
            stat_copy(k, i).start()

    def near_copy(k, i):
        ab = (2, 1, 3)[i]
        src, dst = (
            (stat_near.at[0], stat_near.at[i + 1]),
            (stat_near, stat_all.at[ab]),
            (col_sums.at[i + 1], sums_near.at[i + 1]),
            (sums_near.at[:, ab], sums_all.at[ab]),
        )[k]
        return remote(src, dst, ns.at[k, i], nr.at[k, i], rounds[k % 2][i])

    def near_start(k):
        for i in range(3):
            near_copy(k, i).start()

    def near_finish(k):
        for i in range(3):
            near_copy(k, i).wait_recv()

    def stat_finish(k):
        pairs = []
        for i in range(3):
            stat_copy(k, i).wait_recv()
            pairs.append((stat_in[k, i, :, 0:1], stat_in[k, i, :, 64:65]))
        return pairs

    def multiply(p, dc):
        def step(t, carry):
            da, db, dz = t // 4, (t // 2) % 2, t % 2
            s = t * 2 + dc
            places = (t, 4 * db + 2 * dz + da, 4 * dz + 2 * da + db)

            def put(value, columns):
                for q in range(3):
                    at, size = CUTS[p][q]
                    part[p, q, dc, places[q], 0:size, columns] = value[at : at + size]

            if p == 0:
                put(jnp.dot(both[1, 0:256], held[p, s], preferred_element_type=F32).astype(BF16), slice(0, 256))
            else:
                value = jnp.dot(both[0], held[p, s], preferred_element_type=F32)
                put(value[0:256].astype(BF16), slice(0, 256))
                col_sums[dc + 2 * dz, da * 2 + db, p : p + 1] = value[256:257]
            if p == 1:

                @pl.when(((z + dz) % 2) * ((c + dc) % 2) == 1)
                def _():
                    put(jnp.dot(both[1, 0:256], held[p, s, :, RIGHT], preferred_element_type=F32).astype(BF16), RIGHT)

            return carry

        lax.fori_loop(0, 8, step, 0, unroll=4)

    def stage(p, q, k):
        size = CUTS[p][q][1]
        sem = (rs.at[p, q, k], rr.at[p, q, k])
        if k == 0:
            return remote(part.at[p, q, 1, :, 0:size], got0.at[p, q, :, 0:size], *sem, {"mx": peers[3]})
        slots = 8 >> k
        target = (None, got1, got2, got3)[k]
        return remote(
            part.at[p, q, 0, pl.ds(slots, slots), 0:size], target.at[p, q, :, 0:size], *sem,
            {"mx": peers[SEQ[q][k - 1]]},
        )

    def begin(p):
        for q in range(3):
            stage(p, q, 0).start()

    def advance(p, k):
        source = (got0, got1, got2, got3)[k]
        for q in range(3):
            at, size = CUTS[p][q]
            stage(p, q, k).wait_recv()

            def step(t, carry):
                total = part[p, q, 0, t, 0:size].astype(F32) + source[p, q, t, 0:size].astype(F32)
                part[p, q, 0, t, 0:size] = total.astype(BF16)
                return carry

            if k < 3:
                lax.fori_loop(0, 8 >> k, step, 0, unroll=2)
                stage(p, q, k + 1).start()
            else:
                proj[p, at : at + size] = (
                    part[p, q, 0, 0, 0:size].astype(F32) + source[p, q, 0, 0:size].astype(F32)
                )

    half, piece = x % 2, pl.ds(pl.multiple_of((x // 2) * 48, 48), 48)

    def turn(side, full):
        quarter = full[pl.ds(pl.multiple_of(half * 128, 128), 128), :]
        turned[side] = quarter.T.reshape(4, 96, 128)
        for i in range(3):
            swap(side, i).start()
        mixed[side, 0] = turned[side, r, piece]

    def swap(side, i):
        q = rpeers[i]
        return remote(turned.at[side, q, piece], mixed.at[side, 3 - i], es.at[side, i], er.at[side, i], {"dp": q})

    def pass_on(side, k):
        sem = (fs.at[side, k], fr.at[side, k])
        if k == 0:
            return remote(mixed.at[side], spread.at[side, :, 2], *sem, {"mx": peers[0]})
        if k == 1:
            return remote(mixed.at[side], spread.at[side, :, 1], *sem, {"mx": peers[1]})
        if k == 2:
            return remote(spread.at[side, 0:2, 2], spread.at[side, 0:2, 3], *sem, {"mx": peers[1]})
        return remote(spread.at[side, 2:4, 1], spread.at[side, 2:4, 3], *sem, {"mx": peers[0]})

    def pass_first(side):
        for i in range(3):
            swap(side, i).wait_recv()
        pass_on(side, 0).start()
        pass_on(side, 1).start()
        spread[side, :, 0] = mixed[side]

    def pass_second(side):
        pass_on(side, 0).wait_recv()
        pass_on(side, 2).start()
        pass_on(side, 1).wait_recv()
        pass_on(side, 3).start()

    def left_at(side, q):
        rows_of = pl.ds(pl.multiple_of((q // 2) * 48, 48), 48)
        return left.at[side, 0, :, :, rows_of, lanes(q % 2)]

    def left_send(side, i):
        return remote(spread.at[side], left_at(side, x), ls.at[side, i], lr.at[side, i], {"my": xpeers[i]})

    def left_core(side):
        return remote(left.at[side, 0], left.at[side, 1], ls.at[side, 3], lr.at[side, 3], {"mx": peers[3]})

    def pass_third(side):
        pass_on(side, 2).wait_recv()
        pass_on(side, 3).wait_recv()
        for i in range(3):
            left_send(side, i).start()
        left[side, 0, :, :, piece, lanes(half)] = spread[side]

    def left_here(side):
        for i in range(3):
            q = (x + 3 - i) % 4
            remote(spread.at[side], left_at(side, q), ls.at[side, i], lr.at[side, i], {"my": xpeers[i]}).wait_recv()
        left_core(side).start()

    top, bottom = pl.ds(0, 128), pl.ds(128, 128)

    def hop(p, k, way):
        sem = (zs.at[p, k, way], zr.at[p, k, way])
        if way == 0:
            src = down.at[p] if k == 0 else ring.at[8 - k, p]
            dst = ring.at[7 - k, p]
            if k == 3:
                src, dst = src.at[top], dst.at[top]
            return remote(src, dst, *sem, up)
        src = down.at[p] if k == 0 else ring.at[k, p]
        dst = ring.at[k + 1, p]
        if k == 3:
            src, dst = src.at[bottom], dst.at[bottom]
        return remote(src, dst, *sem, below)

    def hop_start(p, k):
        hop(p, k, 0).start()
        hop(p, k, 1).start()

    def hop_wait(p, k):
        hop(p, k, 0).wait_recv()
        hop(p, k, 1).wait_recv()

    def share(p, dz):
        return down.at[p] if dz == 0 else ring.at[1 + 6 * z, p]

    def y_send(p, dz, k):
        sem = (ys.at[p, dz, k], yr.at[p, dz, k])
        if k == 0:
            return remote(share(p, dz), slots.at[dz, 2, 0, p], *sem, {"mx": peers[0]})
        if k == 1:
            return remote(share(p, dz), slots.at[dz, 1, 0, p], *sem, {"mx": peers[1]})
        if k == 2:
            return remote(slots.at[dz, 2, 0, p, top], slots.at[dz, 3, 0, p, top], *sem, {"mx": peers[1]})
        return remote(slots.at[dz, 1, 0, p, bottom], slots.at[dz, 3, 0, p, bottom], *sem, {"mx": peers[0]})

    def core_send(p, dz, ab):
        src = slots.at[dz, ab, 0, p] if ab else share(p, dz)
        return remote(src, slots.at[dz, ab, 1, p], cs.at[p, dz, ab], cr.at[p, dz, ab], {"mx": peers[3]})

    def spread_share(p, dz):
        y_send(p, dz, 0).start()
        y_send(p, dz, 1).start()
        core_send(p, dz, 0).start()

    def pass_share(p, dz):
        y_send(p, dz, 0).wait_recv()
        y_send(p, dz, 2).start()
        core_send(p, dz, 2).start()
        y_send(p, dz, 1).wait_recv()
        y_send(p, dz, 3).start()
        core_send(p, dz, 1).start()

    def last_share(p, dz):
        y_send(p, dz, 2).wait_recv()
        y_send(p, dz, 3).wait_recv()
        core_send(p, dz, 3).start()

    def dgrad(data, dz, ab, dc):
        s = ab * 4 + dz * 2 + dc
        fourth = ((z + dz) % 2) * ((c + dc) % 2)
        values = jnp.concatenate([data[0, :, LEFT], data[1, :, LEFT]], axis=1)
        acc[0] += dot_last(values, held[0, s])
        acc[1] += dot_last(data[0, :, RIGHT], held[1, s, :, LEFT]) + dot_last(data[2], held[2, s])
        acc[1 - fourth] += dot_last(data[1, :, RIGHT], held[1, s, :, RIGHT])

    def use(dz, ab):
        dgrad(slots.at[dz, ab, 0], dz, ab, 0)

    def use_other(dz, ab):
        for p in range(3):
            core_send(p, dz, ab).wait_recv()
        dgrad(slots.at[dz, ab, 1], dz, ab, 1)

    def result(dz, p, dc, ab):
        return remote(
            res.at[dz, p, dc, ab], got.at[dz, p, dc, ab], gs.at[dz, p, dc, ab], gr.at[dz, p, dc, ab], mate(dc, ab)
        )

    def weight_part(dz, p):
        fourth = ((z + dz) % 2) * c

        def total(dc, side, columns):
            sum_of = None
            for k in range(4):
                d = (dz * (1 + 6 * z) + 2 * k) % 8
                term = jnp.dot(
                    left[side, dc, k].reshape(384, 256), ring[d, p, :, columns], preferred_element_type=F32
                )
                sum_of = term if sum_of is None else sum_of + term
            return sum_of.astype(BF16).reshape(4, 96, -1)

        for dc in range(2):
            if p < 2:
                res[dz, p, dc, :, :, LEFT] = total(dc, 1, LEFT)
                res[dz, p, dc, :, :, RIGHT] = total(dc, fourth if p else 0, RIGHT)
            else:
                res[dz, p, dc] = total(dc, 0, slice(0, 256))
        pltpu.make_async_copy(res.at[dz, p, 0, 0], got.at[dz, p, 0, 0], osem).start()
        for dc, ab in mates:
            result(dz, p, dc, ab).start()

    def x_send(i):
        rows_of = pl.ds(pl.multiple_of(xpeers[i] * 64, 64), 64)
        return remote(xsend.at[:, rows_of], xgot.at[i], xs.at[2, i], xr.at[2, i], {"my": xpeers[i]})

    def settle(p):
        sub = lax.broadcasted_iota(jnp.int32, (128, 256), 0) % 8
        moved = jnp.where(sub == p, stat_all[...].reshape(128, 256) - row_mean, 0.0)
        shift = lax.dot_general(
            moved, sums_all[...].reshape(128, 256), (((0,), (0,)), ((), ())),
            precision=lax.Precision.HIGHEST, preferred_element_type=F32,
        )
        scaled = (proj[p] + shift) * stat_cols[:, 1:2]
        if p == 1:
            keep = jnp.logical_and(
                z * 2 + c == 3, lax.broadcasted_iota(jnp.int32, (256, 256), 1) >= 128
            )
            scaled = jnp.where(keep, proj[p], scaled)
        proj[p] = scaled

    load_weights(1, refs, held, wsem, y, z, c)
    gathered(0, both.at[1])
    wait_weights(0, held, wsem)
    multiply(0, 1)
    begin(0)
    turn(1, both.at[1])
    load_weights(2, refs, held, wsem, y, z, c)
    gathered(3, row_stats)
    across = row_stats[...].T
    stat_near[0] = jnp.where(lax.broadcasted_iota(jnp.int32, (8, 256), 0) < 4, across[0:8], across[64:72])
    near_start(0)
    gathered(1, both.at[0])
    wait_weights(1, held, wsem)
    multiply(1, 1)
    begin(1)
    multiply(0, 0)
    advance(0, 0)
    pass_first(1)
    multiply(1, 0)
    near_finish(0)
    near_start(1)
    wait_weights(2, held, wsem)
    multiply(2, 1)
    begin(2)
    pass_second(1)
    advance(1, 0)
    multiply(2, 0)
    sums_near[0] = col_sums[0]
    near_start(2)
    advance(0, 1)
    advance(2, 0)

    stat_all[0] = stat_near[...]
    near_finish(1)
    sub = lax.broadcasted_iota(jnp.int32, (128, 256), 0) % 8
    every = stat_all[...].reshape(128, 256)
    row_mean = jnp.sum(jnp.where(sub == 0, every, 0.0), axis=0, keepdims=True) / 16
    apart = jnp.where(sub == 0, every - row_mean, 0.0)
    row_square = jnp.sum(jnp.where(sub == 4, every, 0.0) + 384.0 * apart * apart, axis=0, keepdims=True)
    row_inverse = lax.rsqrt(row_square / WIDTH + EPS)
    first_row = lax.broadcasted_iota(jnp.int32, (128, 256), 0) == 0
    stat_cols[...] = jnp.where(first_row, row_mean, row_inverse).T
    inverse = stat_cols[own, 1:2]
    unit = (rows - stat_cols[own, 0:1]) * inverse
    hat[...] = unit
    nown[1] = unit.astype(BF16)
    to_rows(4, nown.at[1], both.at[2])
    near_finish(2)
    near_start(3)
    advance(1, 1)
    advance(0, 2)
    gathered(4, both.at[2])

    turn(0, both.at[2])
    pass_third(1)
    advance(2, 1)
    advance(1, 2)
    advance(0, 3)
    pass_first(0)
    sums_all[0] = sums_near[:, 0]
    near_finish(3)
    advance(1, 3)
    settle(1)

    hidden_unit(proj, down, (1, LEFT), (0, LEFT), (0, LEFT), (0, RIGHT))
    hop_start(0, 0)
    spread_share(0, 0)
    ring[0, 0] = down[0]
    pass_second(0)
    advance(2, 2)
    acc[...] = jnp.zeros_like(acc)
    advance(2, 3)
    settle(2)
    pass_third(0)
    middle(proj, down, z * 2 + c == 3)
    left_here(1)
    hop_wait(0, 0)
    hop_start(0, 1)
    spread_share(0, 1)
    pass_share(0, 0)

    for p in (1, 2):
        hop_start(p, 0)
    for p in (1, 2):
        spread_share(p, 0)
    ring[0, 1:3] = down[1:3]
    hop_wait(0, 1)
    hop_start(0, 2)
    pass_share(0, 1)
    last_share(0, 0)
    hop_wait(1, 0)
    hop_start(1, 1)
    spread_share(1, 1)
    hop_wait(2, 0)
    spread_share(2, 1)
    dgrad(down, 0, 0, 0)
    hop_wait(0, 2)
    hop_start(0, 3)
    left_here(0)
    for p in (1, 2):
        pass_share(p, 0)
    hop_wait(1, 1)
    hop_start(1, 2)
    hop_start(2, 1)
    last_share(0, 1)
    use_other(0, 0)
    hop_wait(0, 3)
    for side in range(2):
        left_core(side).wait_recv()
    for p in (1, 2):
        pass_share(p, 1)
    weight_part(0, 0)
    weight_part(1, 0)
    hop_wait(1, 2)
    hop_start(1, 3)
    hop_wait(2, 1)
    hop_start(2, 2)
    for p in (1, 2):
        last_share(p, 0)
    dgrad(ring.at[1 + 6 * z], 1, 0, 0)
    use(0, 2)
    use(0, 1)
    hop_wait(1, 3)
    weight_part(0, 1)
    weight_part(1, 1)
    hop_wait(2, 2)
    hop_start(2, 3)
    for p in (1, 2):
        last_share(p, 1)
    use_other(1, 0)
    use(0, 3)
    use_other(0, 2)
    use_other(0, 1)
    use(1, 2)
    use(1, 1)
    hop_wait(2, 3)
    weight_part(0, 2)
    weight_part(1, 2)
    use(1, 3)
    use_other(0, 3)
    for ab in (2, 1, 3):
        use_other(1, ab)

    xsend[...] = acc[...].astype(BF16)
    for i in range(3):
        x_send(i).start()
    own = pl.ds(pl.multiple_of(x * 64, 64), 64)
    branch = acc[0, own, :]
    grad = acc[1, own, :]
    for i in range(3):
        x_send(i).wait_recv()
        branch = branch + xgot[i, 0].astype(F32)
        grad = grad + xgot[i, 1].astype(F32)
    outputs[...] = (inp[...].astype(F32) + branch).astype(BF16)
    unit = hat[...]
    sums = (jnp.sum(grad, axis=1, keepdims=True), jnp.sum(grad * unit, axis=1, keepdims=True))
    for k in (2, 3):
        stat_start(k, sums)
        for pair in stat_finish(k):
            sums = (sums[0] + pair[0], sums[1] + pair[1])
    fixed = (grad - sums[0] / WIDTH - unit * (sums[1] / WIDTH)) * inverse
    block_grad[...] = (cot[...].astype(F32) + fixed).astype(BF16)

    parts = [(dz, p) for p in range(3) for dz in range(2)]
    for dz, p in parts:
        for dc, ab in mates:
            result(dz, p, dc, ab).wait_recv()
    for copy in sends:
        copy.wait_send()
    for k in range(4):
        for side in range(2):
            pass_on(side, k).wait_send()
        for i in range(3):
            near_copy(k, i).wait_send()
            if k > 1:
                stat_copy(k, i).wait_send()
    for p in range(3):
        for q in range(3):
            for k in range(4):
                stage(p, q, k).wait_send()
    for p in range(3):
        for k in range(4):
            for way in range(2):
                hop(p, k, way).wait_send()
            for dz in range(2):
                y_send(p, dz, k).wait_send()
                core_send(p, dz, k).wait_send()
    for i in range(3):
        x_send(i).wait_send()
        for side in range(2):
            left_send(side, i).wait_send()
            swap(side, i).wait_send()
    for side in range(2):
        left_core(side).wait_send()
    for dz, p in parts:
        for dc, ab in mates:
            result(dz, p, dc, ab).wait_send()
    pltpu.make_async_copy(res.at[:, :, 0, 0], got.at[:, :, 0, 0], osem).wait()


def deliver_kernel(got, outputs, block_grad, out, grad_out, tgrad, egrad, mgrad, sgrad, sem):
    r, m, x, y, z, c = place()
    grads = named(tgrad, egrad, mgrad, sgrad)
    out[...] = outputs[...]
    grad_out[...] = block_grad[...]

    def step(w, carry):
        dz, dc, ab = w // 8, (w // 4) % 2, w % 4
        fourth, usual, last = share_columns(*owner_of(y, z, c, ab // 2, ab % 2, dz, dc))

        def start(blocks):
            for j in range(6):
                name, index = blocks[PAIRS[j // 2][j % 2]]
                pltpu.make_async_copy(
                    got.at[dz, j // 2, dc, ab, :, pl.ds(128 * (j % 2), 128)], grads[name].at[:, lanes(index)], sem
                ).start()

        @pl.when(fourth)
        def _():
            start(last)

        @pl.when(jnp.logical_not(fourth))
        def _():
            start(usual)

        return carry

    lax.fori_loop(0, 16, step, 0)
    pltpu.make_async_copy(got, got, sem).wait()


def params(number=None):
    if number is None:
        return pltpu.CompilerParams(vmem_limit_bytes=VMEM_LIMIT)
    return pltpu.CompilerParams(collective_id=number, has_side_effects=True, vmem_limit_bytes=VMEM_LIMIT)


VM = pl.BlockSpec(memory_space=pltpu.VMEM)
HB = pl.BlockSpec(memory_space=pl.ANY)
SEM = pltpu.SemaphoreType.DMA


def shape(*dims, dtype=BF16):
    return jax.ShapeDtypeStruct(dims, dtype)


def block(inp, cot, tri, exp, mer, shr):
    return pl.pallas_call(
        block_kernel,
        out_shape=(shape(64, 384), shape(64, 384), shape(2, 3, 2, 4, 96, 256)),
        in_specs=[VM, VM, HB, HB, HB, HB],
        out_specs=(VM, VM, HB),
        scratch_shapes=[
            pltpu.VMEM((3, 16, 384, 256), BF16),
            pltpu.VMEM((3, 3, 2, 8, 96, 256), BF16),
            pltpu.VMEM((3, 3, 8, 96, 256), BF16),
            pltpu.VMEM((3, 3, 4, 96, 256), BF16),
            pltpu.VMEM((3, 3, 2, 96, 256), BF16),
            pltpu.VMEM((3, 3, 1, 96, 256), BF16),
            pltpu.VMEM((4, 64, 128), F32),
            pltpu.VMEM((4, 3, 64, 128), F32),
            pltpu.VMEM((256, 128), F32),
            pltpu.VMEM((64, 128), F32),
            pltpu.VMEM((4, 8, 256), F32),
            pltpu.VMEM((4, 4, 8, 256), F32),
            pltpu.VMEM((4, 4, 8, 256), F32),
            pltpu.VMEM((4, 4, 8, 256), F32),
            pltpu.VMEM((4, 4, 8, 256), F32),
            pltpu.VMEM((256, 128), F32),
            pltpu.VMEM((2, 64, 384), BF16),
            pltpu.VMEM((3, 272, 384), BF16),
            pltpu.VMEM((2, 4, 96, 128), BF16),
            pltpu.VMEM((2, 4, 48, 128), BF16),
            pltpu.VMEM((2, 4, 4, 48, 128), BF16),
            pltpu.VMEM((64, 384), F32),
            pltpu.VMEM((3, 256, 256), F32),
            pltpu.VMEM((3, 256, 256), BF16),
            pltpu.VMEM((2, 4, 2, 3, 256, 256), BF16),
            pltpu.VMEM((2, 256, 384), F32),
            pltpu.VMEM((2, 256, 384), BF16),
            pltpu.VMEM((3, 2, 64, 384), BF16),
            pltpu.VMEM((8, 3, 256, 256), BF16),
            pltpu.VMEM((2, 2, 4, 4, 96, 256), BF16),
            pltpu.VMEM((2, 3, 2, 4, 96, 256), BF16),
            SEM((3,)), SEM((5, 3)), SEM((5, 3)), SEM((4, 3)), SEM((4, 3)), SEM((4, 3)), SEM((4, 3)), SEM((3, 3, 4)), SEM((3, 3, 4)),
            SEM((2, 3)), SEM((2, 3)), SEM((2, 4)), SEM((2, 4)),
            SEM((3, 4, 2)), SEM((3, 4, 2)), SEM((3, 2, 4)), SEM((3, 2, 4)), SEM((3, 2, 4)), SEM((3, 2, 4)),
            SEM((2, 4)), SEM((2, 4)), SEM((2, 3, 2, 4)), SEM((2, 3, 2, 4)), SEM(()),
        ],
        compiler_params=params(0),
        name="block",
    )(inp, cot, tri, exp, mer, shr)


def deliver(got, outputs, block_grad):
    return pl.pallas_call(
        deliver_kernel,
        out_shape=(
            shape(64, 384), shape(64, 384), shape(3, 96, 1536), shape(96, 3072), shape(96, 1536), shape(96, 3072),
        ),
        in_specs=[VM] * 3,
        out_specs=(VM, VM) + (HB,) * 4,
        scratch_shapes=[SEM(())],
        compiler_params=params(),
        name="deliver",
    )(got, outputs, block_grad)


def body(inputs, triple_weight, expand_weight, merge_weight, shrink_weight, cotangent):
    weights = (triple_weight.transpose(1, 0, 2), expand_weight, merge_weight, shrink_weight)
    outputs, block_grad, got = block(inputs, cotangent, *weights)
    outputs, block_grad, tg, eg, mg, sg = deliver(got, outputs, block_grad)
    return outputs, block_grad, tg.transpose(1, 0, 2), eg, mg, sg


def solution(mesh):
    placed = (
        P(("dp", "my"), "mx"),
        P("mx", None, "my"),
        P("mx", "my"),
        P("mx", "my"),
        P("mx", "my"),
        P(("dp", "my"), "mx"),
    )
    return jax.shard_map(
        body,
        mesh=mesh,
        in_specs=placed,
        out_specs=(
            P(("dp", "my"), "mx"),
            P(("dp", "my"), "mx"),
            P(("mx", "dp"), None, "my"),
            P(("mx", "dp"), "my"),
            P(("mx", "dp"), "my"),
            P(("mx", "dp"), "my"),
        ),
        check_vma=False,
    )
```

```python
import math

import jax
import jax.numpy as jnp
from jax import lax
from jax.experimental import pallas as pl
from jax.experimental.pallas import tpu as pltpu
from jax.sharding import PartitionSpec as P

MESH = pl.DeviceIdType.MESH
F32 = jnp.float32
BF16 = jnp.bfloat16

WIDTH = 6144
EPS = 1e-06
ROOT_HALF = 0.7071067811865476
INV_ROOT_TAU = 0.3989422804014327
SCALE = 1.0 / math.sqrt(128)
VMEM_LIMIT = 60 * 1024 * 1024

SEQ = ((0, 1, 2), (1, 2, 0), (2, 0, 1))
PAIRS = ((0, 2), (1, 3), (4, 5))
CUTS = (((0, 96), (96, 80), (176, 80)), ((0, 80), (80, 96), (176, 80)), ((0, 80), (80, 80), (160, 96)))


def place():
    m = lax.axis_index("mx")
    c = m % 2
    y = (m // 2) % 4
    z = m // 8
    return lax.axis_index("dp"), m, lax.axis_index("my"), y, z, c


def partners(m, y, z, c):
    return (m + 2 * (1 - 2 * (y % 2)), m + 2 * (3 - 2 * y), m + 8 - 16 * z, m + 1 - 2 * c)


def owner_of(y, z, c, da, db, dz, dc):
    b = (y // 2 + db) % 2
    a = (y + y // 2 + da) % 2
    return 2 * b + (a + b) % 2, (z + dz) % 2, (c + dc) % 2


def share_columns(yo, zo, co):
    k = zo * 2 + co
    head = 3 * yo + k
    unit = 6 * yo + k
    usual = (("s", unit), ("m", head), ("e", unit), ("q", head), ("k", head), ("v", head))
    first = 6 * yo + 3
    fourth = (("s", first), ("s", first + 1), ("e", first), ("s", first + 2), ("e", first + 1), ("e", first + 2))
    return k == 3, usual, fourth


def named(tri, exp, mer, shr):
    return {"q": tri.at[0], "k": tri.at[1], "v": tri.at[2], "e": exp, "m": mer, "s": shr}


def lanes(index):
    return pl.ds(pl.multiple_of(index * 128, 128), 128)


def load_weights(p, refs, held, sem, y, z, c):
    def step(s, carry):
        yo, zo, co = owner_of(y, z, c, s // 8, (s // 4) % 2, (s // 2) % 2, s % 2)
        fourth, usual, last = share_columns(yo, zo, co)

        def start(blocks):
            for half in range(2):
                name, index = blocks[2 * p + half]
                pltpu.make_async_copy(
                    refs[name].at[:, lanes(index)], held.at[p, s, :, pl.ds(128 * half, 128)], sem.at[p]
                ).start()

        @pl.when(fourth)
        def _():
            start(last)

        @pl.when(jnp.logical_not(fourth))
        def _():
            start(usual)

        return carry

    lax.fori_loop(0, 16, step, 0)


def wait_weights(p, held, sem):
    pltpu.make_async_copy(held.at[p], held.at[p], sem.at[p]).wait()


def remote(src, dst, send, recv, device):
    return pltpu.make_async_remote_copy(
        src_ref=src, dst_ref=dst, send_sem=send, recv_sem=recv, device_id=device, device_id_type=MESH
    )


def greet(devices):
    barrier = pltpu.get_barrier_semaphore()
    for device in devices:
        pl.semaphore_signal(barrier, inc=1, device_id=device, device_id_type=MESH)
    pl.semaphore_wait(barrier, len(devices))


def dot_last(left, right):
    return lax.dot_general(left, right, (((1,), (1,)), ((), ())), preferred_element_type=F32)


def dot_first(left, right):
    return lax.dot_general(left, right, (((0,), (0,)), ((), ())), preferred_element_type=F32)


def norm_heads(block):
    centre = block - jnp.mean(block, axis=-1, keepdims=True)
    inverse = lax.rsqrt(jnp.mean(centre * centre, axis=-1, keepdims=True) + EPS)
    return centre * inverse, inverse


def norm_backward(grad, unit, inverse):
    first = jnp.mean(grad, axis=-1, keepdims=True)
    second = jnp.mean(grad * unit, axis=-1, keepdims=True)
    return (grad - first - unit * second) * inverse


def gelu_pair(pre):
    phi = 0.5 * (1.0 + lax.erf(pre * ROOT_HALF))
    return pre * phi, phi + pre * jnp.exp(-0.5 * pre * pre) * INV_ROOT_TAU


LEFT = slice(0, 128)
RIGHT = slice(128, 256)


def hidden_unit(proj, out, pre_at, grad_at, value_to, slope_to):
    value, slope = gelu_pair(proj[pre_at[0], :, pre_at[1]])
    grad = proj[grad_at[0], :, grad_at[1]]
    out[value_to[0], :, value_to[1]] = value.astype(BF16)
    out[slope_to[0], :, slope_to[1]] = (grad * slope).astype(BF16)


def middle(proj, out, fourth):
    @pl.when(fourth)
    def _():
        hidden_unit(proj, out, (2, LEFT), (0, RIGHT), (1, LEFT), (2, LEFT))
        hidden_unit(proj, out, (2, RIGHT), (1, RIGHT), (1, RIGHT), (2, RIGHT))

    @pl.when(jnp.logical_not(fourth))
    def _():
        qhat, qinv = norm_heads(proj[1, :, RIGHT])
        khat, kinv = norm_heads(proj[2, :, LEFT])
        q, k = qhat.astype(BF16), khat.astype(BF16)
        v = proj[2, :, RIGHT].astype(BF16)
        datt = proj[0, :, RIGHT].astype(BF16)
        expo = jnp.exp(dot_last(q, k) * SCALE)
        probs = expo / jnp.sum(expo, axis=-1, keepdims=True)
        half = probs.astype(BF16)
        out[1, :, LEFT] = jnp.dot(half, v, preferred_element_type=F32).astype(BF16)
        g = dot_last(datt, v)
        ds = (probs * (g - jnp.sum(probs * g, axis=-1, keepdims=True))).astype(BF16)
        dqn = jnp.dot(ds, k, preferred_element_type=F32) * SCALE
        dkn = dot_first(ds, q) * SCALE
        out[1, :, RIGHT] = norm_backward(dqn, qhat, qinv).astype(BF16)
        out[2, :, LEFT] = norm_backward(dkn, khat, kinv).astype(BF16)
        out[2, :, RIGHT] = dot_first(half, datt).astype(BF16)


def block_kernel(
    inp, cot, tri, exp, mer, shr, outputs, block_grad, got,
    held, part, got0, got1, got2, got3, stat_out, stat_in, row_stats, local, stat_near, stat_all, col_sums, sums_near,
    sums_all, stat_cols, nown, both, turned, mixed, spread, hat, proj, down,
    slots, acc, xsend, xgot, ring, left, res,
    wsem, xs, xr, ss, sr, ns, nr, rs, rr, es, er, fs, fr, zs, zr, ys, yr, cs, cr, ls, lr, gs, gr, osem,
):
    r, m, x, y, z, c = place()
    refs = named(tri, exp, mer, shr)
    peers = partners(m, y, z, c)
    xpeers = [(x + i) % 4 for i in (1, 2, 3)]
    rpeers = [(r + i) % 4 for i in (1, 2, 3)]
    inner = m % 8
    up = {"dp": (r + z) % 4, "mx": inner + 8 * (1 - z)}
    below = {"dp": (r + 3 + z) % 4, "mx": inner + 8 * (1 - z)}
    other_core = 1 - 2 * c
    opposite = (m + 4) % 8 + 8 * z
    near = (None, peers[1], peers[0], opposite)

    def mate(dc, ab):
        base = m if ab == 0 else near[ab]
        return {"mx": base + other_core if dc else base}

    mates = [(dc, ab) for ab in (3, 2, 1, 0) for dc in (0, 1) if dc or ab]
    rounds = (
        ({"mx": peers[3]}, {"mx": peers[2]}, {"mx": peers[2] + other_core}),
        ({"mx": peers[0]}, {"mx": peers[1]}, {"mx": opposite}),
    )
    load_weights(0, refs, held, wsem, y, z, c)

    rows = inp[...].astype(F32)
    mean = jnp.sum(rows, axis=1, keepdims=True) / rows.shape[1]
    centred = rows - mean
    square = jnp.sum(centred * centred, axis=1, keepdims=True)
    low = lax.broadcasted_iota(jnp.int32, (64, 128), 1) < 64
    nown[0] = centred.astype(BF16)
    local[...] = jnp.where(low, mean, square)
    greet(
        [{"my": q} for q in xpeers] + [{"dp": q} for q in rpeers] + [up, below, rounds[0][2]]
        + [mate(dc, ab) for dc, ab in mates]
    )

    own = pl.ds(pl.multiple_of(x * 64, 64), 64)
    sends = []

    def to_rows(k, src, full):
        for i in range(3):
            copy = remote(src, full.at[own], xs.at[k, i], xr.at[k, i], {"my": xpeers[i]})
            copy.start()
            sends.append(copy)
        full[own, :] = src[...]

    def gathered(k, full):
        for i in range(3):
            rows_of = full.at[pl.ds(pl.multiple_of(((x + 3 - i) % 4) * 64, 64), 64)]
            remote(rows_of, rows_of, xs.at[k, i], xr.at[k, i], {"my": xpeers[i]}).wait_recv()

    to_rows(0, cot, both.at[1])
    to_rows(1, nown.at[0], both.at[0])
    to_rows(3, local, row_stats)
    both[0, 256:272, :] = jnp.ones((16, 384), BF16)
    col_sums[...] = jnp.zeros_like(col_sums)

    def stat_copy(k, i):
        return remote(stat_out.at[k], stat_in.at[k, i], ss.at[k, i], sr.at[k, i], rounds[k % 2][i])

    def stat_start(k, pair):
        stat_out[k] = jnp.where(low, pair[0], pair[1])
        for i in range(3):
            stat_copy(k, i).start()

    def near_copy(k, i):
        ab = (2, 1, 3)[i]
        src, dst = (
            (stat_near.at[0], stat_near.at[i + 1]),
            (stat_near, stat_all.at[ab]),
            (col_sums.at[i + 1], sums_near.at[i + 1]),
            (sums_near.at[:, ab], sums_all.at[ab]),
        )[k]
        return remote(src, dst, ns.at[k, i], nr.at[k, i], rounds[k % 2][i])

    def near_start(k):
        for i in range(3):
            near_copy(k, i).start()

    def near_finish(k):
        for i in range(3):
            near_copy(k, i).wait_recv()

    def stat_finish(k):
        pairs = []
        for i in range(3):
            stat_copy(k, i).wait_recv()
            pairs.append((stat_in[k, i, :, 0:1], stat_in[k, i, :, 64:65]))
        return pairs

    def multiply(p, dc):
        def step(t, carry):
            da, db, dz = t // 4, (t // 2) % 2, t % 2
            s = t * 2 + dc
            places = (t, 4 * db + 2 * dz + da, 4 * dz + 2 * da + db)

            def put(value, columns):
                for q in range(3):
                    at, size = CUTS[p][q]
                    part[p, q, dc, places[q], 0:size, columns] = value[at : at + size]

            if p == 0:
                put(jnp.dot(both[1, 0:256], held[p, s], preferred_element_type=F32).astype(BF16), slice(0, 256))
            else:
                value = jnp.dot(both[0], held[p, s], preferred_element_type=F32)
                put(value[0:256].astype(BF16), slice(0, 256))
                col_sums[dc + 2 * dz, da * 2 + db, p : p + 1] = value[256:257]
            if p == 1:

                @pl.when(((z + dz) % 2) * ((c + dc) % 2) == 1)
                def _():
                    put(jnp.dot(both[1, 0:256], held[p, s, :, RIGHT], preferred_element_type=F32).astype(BF16), RIGHT)

            return carry

        lax.fori_loop(0, 8, step, 0, unroll=4)

    def stage(p, q, k):
        size = CUTS[p][q][1]
        sem = (rs.at[p, q, k], rr.at[p, q, k])
        if k == 0:
            return remote(part.at[p, q, 1, :, 0:size], got0.at[p, q, :, 0:size], *sem, {"mx": peers[3]})
        slots = 8 >> k
        target = (None, got1, got2, got3)[k]
        return remote(
            part.at[p, q, 0, pl.ds(slots, slots), 0:size], target.at[p, q, :, 0:size], *sem,
            {"mx": peers[SEQ[q][k - 1]]},
        )

    def begin(p):
        for q in range(3):
            stage(p, q, 0).start()

    def advance(p, k):
        source = (got0, got1, got2, got3)[k]
        for q in range(3):
            at, size = CUTS[p][q]
            stage(p, q, k).wait_recv()

            def step(t, carry):
                total = part[p, q, 0, t, 0:size].astype(F32) + source[p, q, t, 0:size].astype(F32)
                part[p, q, 0, t, 0:size] = total.astype(BF16)
                return carry

            if k < 3:
                lax.fori_loop(0, 8 >> k, step, 0, unroll=2)
                stage(p, q, k + 1).start()
            else:
                proj[p, at : at + size] = (
                    part[p, q, 0, 0, 0:size].astype(F32) + source[p, q, 0, 0:size].astype(F32)
                )

    half, piece = x % 2, pl.ds(pl.multiple_of((x // 2) * 48, 48), 48)

    def turn(side, full):
        quarter = full[pl.ds(pl.multiple_of(half * 128, 128), 128), :]
        turned[side] = quarter.T.reshape(4, 96, 128)
        for i in range(3):
            swap(side, i).start()
        mixed[side, 0] = turned[side, r, piece]

    def swap(side, i):
        q = rpeers[i]
        return remote(turned.at[side, q, piece], mixed.at[side, 3 - i], es.at[side, i], er.at[side, i], {"dp": q})

    def pass_on(side, k):
        sem = (fs.at[side, k], fr.at[side, k])
        if k == 0:
            return remote(mixed.at[side], spread.at[side, :, 2], *sem, {"mx": peers[0]})
        if k == 1:
            return remote(mixed.at[side], spread.at[side, :, 1], *sem, {"mx": peers[1]})
        if k == 2:
            return remote(spread.at[side, 0:2, 2], spread.at[side, 0:2, 3], *sem, {"mx": peers[1]})
        return remote(spread.at[side, 2:4, 1], spread.at[side, 2:4, 3], *sem, {"mx": peers[0]})

    def pass_first(side):
        for i in range(3):
            swap(side, i).wait_recv()
        pass_on(side, 0).start()
        pass_on(side, 1).start()
        spread[side, :, 0] = mixed[side]

    def pass_second(side):
        pass_on(side, 0).wait_recv()
        pass_on(side, 2).start()
        pass_on(side, 1).wait_recv()
        pass_on(side, 3).start()

    def left_at(side, q):
        rows_of = pl.ds(pl.multiple_of((q // 2) * 48, 48), 48)
        return left.at[side, 0, :, :, rows_of, lanes(q % 2)]

    def left_send(side, i):
        return remote(spread.at[side], left_at(side, x), ls.at[side, i], lr.at[side, i], {"my": xpeers[i]})

    def left_core(side):
        return remote(left.at[side, 0], left.at[side, 1], ls.at[side, 3], lr.at[side, 3], {"mx": peers[3]})

    def pass_third(side):
        pass_on(side, 2).wait_recv()
        pass_on(side, 3).wait_recv()
        for i in range(3):
            left_send(side, i).start()
        left[side, 0, :, :, piece, lanes(half)] = spread[side]

    def left_here(side):
        for i in range(3):
            q = (x + 3 - i) % 4
            remote(spread.at[side], left_at(side, q), ls.at[side, i], lr.at[side, i], {"my": xpeers[i]}).wait_recv()
        left_core(side).start()

    top, bottom = pl.ds(0, 128), pl.ds(128, 128)

    def hop(p, k, way):
        sem = (zs.at[p, k, way], zr.at[p, k, way])
        if way == 0:
            src = down.at[p] if k == 0 else ring.at[8 - k, p]
            dst = ring.at[7 - k, p]
            if k == 3:
                src, dst = src.at[top], dst.at[top]
            return remote(src, dst, *sem, up)
        src = down.at[p] if k == 0 else ring.at[k, p]
        dst = ring.at[k + 1, p]
        if k == 3:
            src, dst = src.at[bottom], dst.at[bottom]
        return remote(src, dst, *sem, below)

    def hop_start(p, k):
        hop(p, k, 0).start()
        hop(p, k, 1).start()

    def hop_wait(p, k):
        hop(p, k, 0).wait_recv()
        hop(p, k, 1).wait_recv()

    def share(p, dz):
        return down.at[p] if dz == 0 else ring.at[1 + 6 * z, p]

    def y_send(p, dz, k):
        sem = (ys.at[p, dz, k], yr.at[p, dz, k])
        if k == 0:
            return remote(share(p, dz), slots.at[dz, 2, 0, p], *sem, {"mx": peers[0]})
        if k == 1:
            return remote(share(p, dz), slots.at[dz, 1, 0, p], *sem, {"mx": peers[1]})
        if k == 2:
            return remote(slots.at[dz, 2, 0, p, top], slots.at[dz, 3, 0, p, top], *sem, {"mx": peers[1]})
        return remote(slots.at[dz, 1, 0, p, bottom], slots.at[dz, 3, 0, p, bottom], *sem, {"mx": peers[0]})

    def core_send(p, dz, ab):
        src = slots.at[dz, ab, 0, p] if ab else share(p, dz)
        return remote(src, slots.at[dz, ab, 1, p], cs.at[p, dz, ab], cr.at[p, dz, ab], {"mx": peers[3]})

    def spread_share(p, dz):
        y_send(p, dz, 0).start()
        y_send(p, dz, 1).start()
        core_send(p, dz, 0).start()

    def pass_share(p, dz):
        y_send(p, dz, 0).wait_recv()
        y_send(p, dz, 2).start()
        core_send(p, dz, 2).start()
        y_send(p, dz, 1).wait_recv()
        y_send(p, dz, 3).start()
        core_send(p, dz, 1).start()

    def last_share(p, dz):
        y_send(p, dz, 2).wait_recv()
        y_send(p, dz, 3).wait_recv()
        core_send(p, dz, 3).start()

    def dgrad(data, dz, ab, dc):
        s = ab * 4 + dz * 2 + dc
        fourth = ((z + dz) % 2) * ((c + dc) % 2)
        values = jnp.concatenate([data[0, :, LEFT], data[1, :, LEFT]], axis=1)
        acc[0] += dot_last(values, held[0, s])
        acc[1] += dot_last(data[0, :, RIGHT], held[1, s, :, LEFT]) + dot_last(data[2], held[2, s])
        acc[1 - fourth] += dot_last(data[1, :, RIGHT], held[1, s, :, RIGHT])

    def use(dz, ab):
        dgrad(slots.at[dz, ab, 0], dz, ab, 0)

    def use_other(dz, ab):
        for p in range(3):
            core_send(p, dz, ab).wait_recv()
        dgrad(slots.at[dz, ab, 1], dz, ab, 1)

    def result(dz, p, dc, ab):
        return remote(
            res.at[dz, p, dc, ab], got.at[dz, p, dc, ab], gs.at[dz, p, dc, ab], gr.at[dz, p, dc, ab], mate(dc, ab)
        )

    def weight_part(dz, p):
        fourth = ((z + dz) % 2) * c

        def total(dc, side, columns):
            sum_of = None
            for k in range(4):
                d = (dz * (1 + 6 * z) + 2 * k) % 8
                term = jnp.dot(
                    left[side, dc, k].reshape(384, 256), ring[d, p, :, columns], preferred_element_type=F32
                )
                sum_of = term if sum_of is None else sum_of + term
            return sum_of.astype(BF16).reshape(4, 96, -1)

        for dc in range(2):
            if p < 2:
                res[dz, p, dc, :, :, LEFT] = total(dc, 1, LEFT)
                res[dz, p, dc, :, :, RIGHT] = total(dc, fourth if p else 0, RIGHT)
            else:
                res[dz, p, dc] = total(dc, 0, slice(0, 256))
        pltpu.make_async_copy(res.at[dz, p, 0, 0], got.at[dz, p, 0, 0], osem).start()
        for dc, ab in mates:
            result(dz, p, dc, ab).start()

    def x_send(i):
        rows_of = pl.ds(pl.multiple_of(xpeers[i] * 64, 64), 64)
        return remote(xsend.at[:, rows_of], xgot.at[i], xs.at[2, i], xr.at[2, i], {"my": xpeers[i]})

    def settle(p):
        sub = lax.broadcasted_iota(jnp.int32, (128, 256), 0) % 8
        moved = jnp.where(sub == p, stat_all[...].reshape(128, 256) - row_mean, 0.0)
        shift = lax.dot_general(
            moved, sums_all[...].reshape(128, 256), (((0,), (0,)), ((), ())),
            precision=lax.Precision.HIGHEST, preferred_element_type=F32,
        )
        scaled = (proj[p] + shift) * stat_cols[:, 1:2]
        if p == 1:
            keep = jnp.logical_and(
                z * 2 + c == 3, lax.broadcasted_iota(jnp.int32, (256, 256), 1) >= 128
            )
            scaled = jnp.where(keep, proj[p], scaled)
        proj[p] = scaled

    load_weights(1, refs, held, wsem, y, z, c)
    gathered(0, both.at[1])
    wait_weights(0, held, wsem)
    multiply(0, 1)
    begin(0)
    turn(1, both.at[1])
    load_weights(2, refs, held, wsem, y, z, c)
    gathered(3, row_stats)
    across = row_stats[...].T
    stat_near[0] = jnp.where(lax.broadcasted_iota(jnp.int32, (8, 256), 0) < 4, across[0:8], across[64:72])
    near_start(0)
    gathered(1, both.at[0])
    wait_weights(1, held, wsem)
    multiply(1, 1)
    begin(1)
    multiply(0, 0)
    advance(0, 0)
    pass_first(1)
    multiply(1, 0)
    near_finish(0)
    near_start(1)
    wait_weights(2, held, wsem)
    multiply(2, 1)
    begin(2)
    pass_second(1)
    advance(1, 0)
    multiply(2, 0)
    sums_near[0] = col_sums[0]
    near_start(2)
    advance(0, 1)
    advance(2, 0)

    stat_all[0] = stat_near[...]
    near_finish(1)
    sub = lax.broadcasted_iota(jnp.int32, (128, 256), 0) % 8
    every = stat_all[...].reshape(128, 256)
    row_mean = jnp.sum(jnp.where(sub == 0, every, 0.0), axis=0, keepdims=True) / 16
    apart = jnp.where(sub == 0, every - row_mean, 0.0)
    row_square = jnp.sum(jnp.where(sub == 4, every, 0.0) + 384.0 * apart * apart, axis=0, keepdims=True)
    row_inverse = lax.rsqrt(row_square / WIDTH + EPS)
    first_row = lax.broadcasted_iota(jnp.int32, (128, 256), 0) == 0
    stat_cols[...] = jnp.where(first_row, row_mean, row_inverse).T
    inverse = stat_cols[own, 1:2]
    unit = (rows - stat_cols[own, 0:1]) * inverse
    hat[...] = unit
    nown[1] = unit.astype(BF16)
    to_rows(4, nown.at[1], both.at[2])
    near_finish(2)
    near_start(3)
    advance(1, 1)
    advance(0, 2)
    gathered(4, both.at[2])

    turn(0, both.at[2])
    pass_third(1)
    advance(2, 1)
    advance(1, 2)
    advance(0, 3)
    pass_first(0)
    sums_all[0] = sums_near[:, 0]
    near_finish(3)
    advance(1, 3)
    settle(1)

    hidden_unit(proj, down, (1, LEFT), (0, LEFT), (0, LEFT), (0, RIGHT))
    hop_start(0, 0)
    spread_share(0, 0)
    ring[0, 0] = down[0]
    pass_second(0)
    advance(2, 2)
    acc[...] = jnp.zeros_like(acc)
    advance(2, 3)
    settle(2)
    pass_third(0)
    middle(proj, down, z * 2 + c == 3)
    left_here(1)
    hop_wait(0, 0)
    hop_start(0, 1)
    spread_share(0, 1)
    pass_share(0, 0)

    for p in (1, 2):
        hop_start(p, 0)
    for p in (1, 2):
        spread_share(p, 0)
    ring[0, 1:3] = down[1:3]
    hop_wait(0, 1)
    hop_start(0, 2)
    pass_share(0, 1)
    last_share(0, 0)
    hop_wait(1, 0)
    hop_start(1, 1)
    spread_share(1, 1)
    hop_wait(2, 0)
    spread_share(2, 1)
    dgrad(down, 0, 0, 0)
    hop_wait(0, 2)
    hop_start(0, 3)
    left_here(0)
    for p in (1, 2):
        pass_share(p, 0)
    hop_wait(1, 1)
    hop_start(1, 2)
    hop_start(2, 1)
    last_share(0, 1)
    use_other(0, 0)
    hop_wait(0, 3)
    for side in range(2):
        left_core(side).wait_recv()
    for p in (1, 2):
        pass_share(p, 1)
    weight_part(0, 0)
    weight_part(1, 0)
    hop_wait(1, 2)
    hop_start(1, 3)
    hop_wait(2, 1)
    hop_start(2, 2)
    for p in (1, 2):
        last_share(p, 0)
    dgrad(ring.at[1 + 6 * z], 1, 0, 0)
    use(0, 2)
    use(0, 1)
    hop_wait(1, 3)
    weight_part(0, 1)
    weight_part(1, 1)
    hop_wait(2, 2)
    hop_start(2, 3)
    for p in (1, 2):
        last_share(p, 1)
    use_other(1, 0)
    use(0, 3)
    use_other(0, 2)
    use_other(0, 1)
    use(1, 2)
    use(1, 1)
    use(1, 3)
    use_other(0, 3)
    for ab in (2, 1, 3):
        use_other(1, ab)

    xsend[...] = acc[...].astype(BF16)
    for i in range(3):
        x_send(i).start()
    hop_wait(2, 3)
    weight_part(0, 2)
    weight_part(1, 2)
    own = pl.ds(pl.multiple_of(x * 64, 64), 64)
    branch = acc[0, own, :]
    grad = acc[1, own, :]
    for i in range(3):
        x_send(i).wait_recv()
        branch = branch + xgot[i, 0].astype(F32)
        grad = grad + xgot[i, 1].astype(F32)
    outputs[...] = (inp[...].astype(F32) + branch).astype(BF16)
    unit = hat[...]
    sums = (jnp.sum(grad, axis=1, keepdims=True), jnp.sum(grad * unit, axis=1, keepdims=True))
    for k in (2, 3):
        stat_start(k, sums)
        for pair in stat_finish(k):
            sums = (sums[0] + pair[0], sums[1] + pair[1])
    fixed = (grad - sums[0] / WIDTH - unit * (sums[1] / WIDTH)) * inverse
    block_grad[...] = (cot[...].astype(F32) + fixed).astype(BF16)

    parts = [(dz, p) for p in range(3) for dz in range(2)]
    for dz, p in parts:
        for dc, ab in mates:
            result(dz, p, dc, ab).wait_recv()
    for copy in sends:
        copy.wait_send()
    for k in range(4):
        for side in range(2):
            pass_on(side, k).wait_send()
        for i in range(3):
            near_copy(k, i).wait_send()
            if k > 1:
                stat_copy(k, i).wait_send()
    for p in range(3):
        for q in range(3):
            for k in range(4):
                stage(p, q, k).wait_send()
    for p in range(3):
        for k in range(4):
            for way in range(2):
                hop(p, k, way).wait_send()
            for dz in range(2):
                y_send(p, dz, k).wait_send()
                core_send(p, dz, k).wait_send()
    for i in range(3):
        x_send(i).wait_send()
        for side in range(2):
            left_send(side, i).wait_send()
            swap(side, i).wait_send()
    for side in range(2):
        left_core(side).wait_send()
    for dz, p in parts:
        for dc, ab in mates:
            result(dz, p, dc, ab).wait_send()
    pltpu.make_async_copy(res.at[:, :, 0, 0], got.at[:, :, 0, 0], osem).wait()


def deliver_kernel(got, outputs, block_grad, out, grad_out, tgrad, egrad, mgrad, sgrad, sem):
    r, m, x, y, z, c = place()
    grads = named(tgrad, egrad, mgrad, sgrad)
    out[...] = outputs[...]
    grad_out[...] = block_grad[...]

    def step(w, carry):
        dz, dc, ab = w // 8, (w // 4) % 2, w % 4
        fourth, usual, last = share_columns(*owner_of(y, z, c, ab // 2, ab % 2, dz, dc))

        def start(blocks):
            for j in range(6):
                name, index = blocks[PAIRS[j // 2][j % 2]]
                pltpu.make_async_copy(
                    got.at[dz, j // 2, dc, ab, :, pl.ds(128 * (j % 2), 128)], grads[name].at[:, lanes(index)], sem
                ).start()

        @pl.when(fourth)
        def _():
            start(last)

        @pl.when(jnp.logical_not(fourth))
        def _():
            start(usual)

        return carry

    lax.fori_loop(0, 16, step, 0)
    pltpu.make_async_copy(got, got, sem).wait()


def params(number=None):
    if number is None:
        return pltpu.CompilerParams(vmem_limit_bytes=VMEM_LIMIT)
    return pltpu.CompilerParams(collective_id=number, has_side_effects=True, vmem_limit_bytes=VMEM_LIMIT)


VM = pl.BlockSpec(memory_space=pltpu.VMEM)
HB = pl.BlockSpec(memory_space=pl.ANY)
SEM = pltpu.SemaphoreType.DMA


def shape(*dims, dtype=BF16):
    return jax.ShapeDtypeStruct(dims, dtype)


def block(inp, cot, tri, exp, mer, shr):
    return pl.pallas_call(
        block_kernel,
        out_shape=(shape(64, 384), shape(64, 384), shape(2, 3, 2, 4, 96, 256)),
        in_specs=[VM, VM, HB, HB, HB, HB],
        out_specs=(VM, VM, HB),
        scratch_shapes=[
            pltpu.VMEM((3, 16, 384, 256), BF16),
            pltpu.VMEM((3, 3, 2, 8, 96, 256), BF16),
            pltpu.VMEM((3, 3, 8, 96, 256), BF16),
            pltpu.VMEM((3, 3, 4, 96, 256), BF16),
            pltpu.VMEM((3, 3, 2, 96, 256), BF16),
            pltpu.VMEM((3, 3, 1, 96, 256), BF16),
            pltpu.VMEM((4, 64, 128), F32),
            pltpu.VMEM((4, 3, 64, 128), F32),
            pltpu.VMEM((256, 128), F32),
            pltpu.VMEM((64, 128), F32),
            pltpu.VMEM((4, 8, 256), F32),
            pltpu.VMEM((4, 4, 8, 256), F32),
            pltpu.VMEM((4, 4, 8, 256), F32),
            pltpu.VMEM((4, 4, 8, 256), F32),
            pltpu.VMEM((4, 4, 8, 256), F32),
            pltpu.VMEM((256, 128), F32),
            pltpu.VMEM((2, 64, 384), BF16),
            pltpu.VMEM((3, 272, 384), BF16),
            pltpu.VMEM((2, 4, 96, 128), BF16),
            pltpu.VMEM((2, 4, 48, 128), BF16),
            pltpu.VMEM((2, 4, 4, 48, 128), BF16),
            pltpu.VMEM((64, 384), F32),
            pltpu.VMEM((3, 256, 256), F32),
            pltpu.VMEM((3, 256, 256), BF16),
            pltpu.VMEM((2, 4, 2, 3, 256, 256), BF16),
            pltpu.VMEM((2, 256, 384), F32),
            pltpu.VMEM((2, 256, 384), BF16),
            pltpu.VMEM((3, 2, 64, 384), BF16),
            pltpu.VMEM((8, 3, 256, 256), BF16),
            pltpu.VMEM((2, 2, 4, 4, 96, 256), BF16),
            pltpu.VMEM((2, 3, 2, 4, 96, 256), BF16),
            SEM((3,)), SEM((5, 3)), SEM((5, 3)), SEM((4, 3)), SEM((4, 3)), SEM((4, 3)), SEM((4, 3)), SEM((3, 3, 4)), SEM((3, 3, 4)),
            SEM((2, 3)), SEM((2, 3)), SEM((2, 4)), SEM((2, 4)),
            SEM((3, 4, 2)), SEM((3, 4, 2)), SEM((3, 2, 4)), SEM((3, 2, 4)), SEM((3, 2, 4)), SEM((3, 2, 4)),
            SEM((2, 4)), SEM((2, 4)), SEM((2, 3, 2, 4)), SEM((2, 3, 2, 4)), SEM(()),
        ],
        compiler_params=params(0),
        name="block",
    )(inp, cot, tri, exp, mer, shr)


def deliver(got, outputs, block_grad):
    return pl.pallas_call(
        deliver_kernel,
        out_shape=(
            shape(64, 384), shape(64, 384), shape(3, 96, 1536), shape(96, 3072), shape(96, 1536), shape(96, 3072),
        ),
        in_specs=[VM] * 3,
        out_specs=(VM, VM) + (HB,) * 4,
        scratch_shapes=[SEM(())],
        compiler_params=params(),
        name="deliver",
    )(got, outputs, block_grad)


def body(inputs, triple_weight, expand_weight, merge_weight, shrink_weight, cotangent):
    weights = (triple_weight.transpose(1, 0, 2), expand_weight, merge_weight, shrink_weight)
    outputs, block_grad, got = block(inputs, cotangent, *weights)
    outputs, block_grad, tg, eg, mg, sg = deliver(got, outputs, block_grad)
    return outputs, block_grad, tg.transpose(1, 0, 2), eg, mg, sg


def solution(mesh):
    placed = (
        P(("dp", "my"), "mx"),
        P("mx", None, "my"),
        P("mx", "my"),
        P("mx", "my"),
        P("mx", "my"),
        P(("dp", "my"), "mx"),
    )
    return jax.shard_map(
        body,
        mesh=mesh,
        in_specs=placed,
        out_specs=(
            P(("dp", "my"), "mx"),
            P(("dp", "my"), "mx"),
            P(("mx", "dp"), None, "my"),
            P(("mx", "dp"), "my"),
            P(("mx", "dp"), "my"),
            P(("mx", "dp"), "my"),
        ),
        check_vma=False,
    )
```
